32 devices in a mesh: ctx: 16 (over z, y, core), ch: 2 (over x).
Axes of the slice: x: 2, y: 2, z: 4, core: 2. Of those that a mesh axis runs over, the one named last changes fastest.
Arguments:
- streams: bfloat16 [3, 4096, 1024], P(None, 'ctx', 'ch'), may hold values from -6 to 6
- short_weight: float32 [3, 7, 1024], P(None, None, 'ch'), may hold values from -2 to 2
- long_filter: float32 [4096, 1024], P('ctx', 'ch'), may hold values from -32 to 32
- cotangent: bfloat16 [4096, 1024], P('ctx', 'ch'), may hold values from -16 to 16
Outputs:
- hyena_out: bfloat16 [4096, 1024], P('ctx', 'ch')
- stream_grad: bfloat16 [3, 4096, 1024], P(None, 'ctx', 'ch')
- short_grad: float32 [3, 7, 1024], P(None, None, 'ch')
- filter_grad: float32 [4096, 1024], P('ctx', 'ch')
The draws below stay inside these ranges and needn't reach their ends.
All inputs are finite; a program needn't handle non-finite values.
Results may differ from the reference program's by a relative error of at most 0.0014.
Values may be sent and summed in bfloat16 or wider, within the bound.
A program may use at most 128 MiB of HBM per device.

```python
import math
import jax
import jax.numpy as jnp
from jax import lax

FEATURE_WIDTH = 1024
KERNEL = 7
SEQUENCE_LENGTH = 4096


def draw_long_filter(key, part):
    k_jitter, k_kind, k_slow, k_fast, indices_random_key, keeping_random_key = jax.random.split(jax.random.fold_in(key, 11), 6)
    sequence_index = jnp.arange(SEQUENCE_LENGTH, dtype=jnp.float32)[:, None]
    slow_rate = jnp.exp(jax.random.uniform(k_slow, (FEATURE_WIDTH,), jnp.float32, math.log(0.1 / SEQUENCE_LENGTH), math.log(2.0 / SEQUENCE_LENGTH)))
    fast_rate = jnp.exp(jax.random.uniform(k_fast, (FEATURE_WIDTH,), jnp.float32, math.log(2.0 / SEQUENCE_LENGTH), math.log(1.0 / 30.0)))
    slow_share = 0.5
    pick = jax.random.uniform(k_kind, (FEATURE_WIDTH,), jnp.float32)
    attenuation_rate = jnp.where(pick < slow_share, slow_rate, fast_rate)
    spike_indices = jax.random.randint(indices_random_key, (3,), 0, SEQUENCE_LENGTH).astype(jnp.float32)
    passed_spikes = jnp.sum((sequence_index >= spike_indices[None, :]).astype(jnp.float32), axis=1, keepdims=True)
    spike_keep_flags = jax.random.uniform(keeping_random_key, (FEATURE_WIDTH,), jnp.float32, 0.5, 0.8)
    attenuation_multiplier = jnp.exp(-attenuation_rate[None, :] * sequence_index) * jnp.power(spike_keep_flags[None, :], passed_spikes)
    amplitude = jnp.minimum(jnp.sqrt(jnp.maximum(2.0 * attenuation_rate * SEQUENCE_LENGTH, 1.0)), 8.0)
    jitter = jnp.clip(jax.random.normal(k_jitter, (SEQUENCE_LENGTH, FEATURE_WIDTH), jnp.float32), -4.0, 4.0)
    return (jitter * attenuation_multiplier * amplitude[None, :]).astype(jnp.float32)


def draw_cotangent(key, part):
    k_jitter = jax.random.fold_in(key, 23)
    sequence_index = jnp.arange(SEQUENCE_LENGTH, dtype=jnp.float32) / (SEQUENCE_LENGTH - 1)
    growth = 1.0 + 2.0 * sequence_index
    jitter = jnp.clip(jax.random.normal(k_jitter, (SEQUENCE_LENGTH, FEATURE_WIDTH), jnp.float32), -4.0, 4.0)
    return (jitter * growth[:, None]).astype(jnp.bfloat16)


def shard_levels(own_key, dims, pieces, least, top_value):
    def one(axis_at, blocks):
        steps = jax.random.uniform(jax.random.fold_in(jax.random.fold_in(own_key, 6), axis_at), (blocks,), jnp.float32, least / len(pieces), top_value / len(pieces))
        return jnp.repeat(jnp.exp(steps), dims[axis_at] // blocks).reshape((-1,) + (1,) * (len(dims) - axis_at - 1))

    factor_of = one(*pieces[0])
    for cut in pieces[1:]:
        factor_of = factor_of * one(*cut)
    return factor_of


def normal_values(rng, dims, width, reach, cuts=(), kind=jnp.bfloat16):
    entries = jax.random.normal(rng, dims, jnp.float32) * width
    if len(cuts) > 0:
        entries = shard_levels(rng, dims, cuts, -0.22, 0.18) * entries
    return jnp.clip(entries, min=-reach, max=reach).astype(kind)


def setup_inputs(seed: int = 0) -> dict:
    splits = jax.random.split(jax.random.key(seed), 5)
    return {
        "streams": normal_values(splits[0], (3, SEQUENCE_LENGTH, FEATURE_WIDTH), 1.0, 6.0, ((1, 16), (2, 2))),
        "short_weight": normal_values(splits[1], (3, KERNEL, FEATURE_WIDTH), KERNEL ** -0.5, 2.0, ((2, 2),), jnp.float32),
        "long_filter": draw_long_filter(jax.random.fold_in(splits[4], 71), 0),
        "cotangent": draw_cotangent(jax.random.fold_in(splits[4], 71), 0),
    }


def causal_features(streams, short_weight):
    seq_rows = streams.shape[1]
    padded = jnp.pad(streams.astype(jnp.float32), ((0, 0), (KERNEL - 1, 0), (0, 0)))
    features = jnp.zeros(streams.shape, jnp.float32)
    for offset in range(KERNEL):
        start = KERNEL - 1 - offset
        features = features + short_weight[:, offset, None, :] * padded[:, start:start + seq_rows, :]
    return (features, padded)

def reference(streams, short_weight, long_filter, cotangent):
    padded_len = 2 * SEQUENCE_LENGTH
    norm_factor = 1.0 / math.sqrt(SEQUENCE_LENGTH)
    features, padded = causal_features(streams, short_weight)
    product = features[1] * features[2]
    scaled = long_filter * norm_factor
    prod_spec = jnp.fft.rfft(product, n=padded_len, axis=0)
    filt_spec = jnp.fft.rfft(scaled, n=padded_len, axis=0)
    mixed_long = jnp.fft.irfft(prod_spec * filt_spec, n=padded_len, axis=0)[:SEQUENCE_LENGTH]
    hyena_out = (features[0] * mixed_long).astype(jnp.bfloat16)
    grad_out = cotangent.astype(jnp.float32)
    grad_long = grad_out * features[0]
    grad_query = grad_out * mixed_long
    grad_spec = jnp.fft.rfft(grad_long, n=padded_len, axis=0)
    grad_product = jnp.fft.irfft(jnp.conj(filt_spec) * grad_spec, n=padded_len, axis=0)[:SEQUENCE_LENGTH]
    grad_scaled = jnp.fft.irfft(jnp.conj(prod_spec) * grad_spec, n=padded_len, axis=0)[:SEQUENCE_LENGTH]
    filter_grad = grad_scaled * norm_factor
    feature_grad = jnp.stack([grad_query, grad_product * features[2], grad_product * features[1]])
    short_parts = []
    for offset in range(KERNEL):
        start = KERNEL - 1 - offset
        short_parts.append(lax.optimization_barrier(jnp.sum(feature_grad * padded[:, start:start + SEQUENCE_LENGTH, :], axis=1)))
    short_grad = jnp.stack(short_parts, axis=1)
    grad_padded = jnp.pad(feature_grad, ((0, 0), (0, KERNEL - 1), (0, 0)))
    stream_grad = jnp.zeros(feature_grad.shape, jnp.float32)
    for offset in range(KERNEL):
        stream_grad = stream_grad + short_weight[:, offset, None, :] * grad_padded[:, offset:offset + SEQUENCE_LENGTH, :]
    return (hyena_out, stream_grad.astype(jnp.bfloat16), short_grad, filter_grad)
```

```python
import functools
import math

import jax
import jax.numpy as jnp
import numpy as np
from jax import lax
from jax.experimental import pallas as pl
from jax.experimental.pallas import tpu as pltpu
from jax.sharding import PartitionSpec as P

span = 250.0
half_span = 125.0
tiny = 1e-30
f32 = jnp.float32


def passed_along(block, axis, distance):
    devices = range(lax.axis_size(axis))
    route = [(i - distance, i) for i in devices if i - distance in devices]
    return lax.ppermute(block, axis, route)


def encode(values, top):
    power = jnp.abs(values) * (span / top) - half_span
    code = jnp.exp2(power)
    return jnp.where(values < 0.0, -code, code).astype(jnp.bfloat16)


def decode(code, top):
    code = code.astype(f32)
    size = (jnp.log2(jnp.abs(code)) + half_span) * (top * (1.0 / span))
    return jnp.where(code < 0.0, -size, size)


def row_top(values):
    return jnp.maximum(jnp.max(jnp.abs(values), axis=1, keepdims=True), tiny)


def to_lanes(column):
    rows = column.shape[0]
    lane = lax.broadcasted_iota(jnp.int32, (rows, 128), 1)
    row = lax.broadcasted_iota(jnp.int32, (rows, 128), 0)
    return jnp.sum(jnp.where(lane == row, column, 0.0), axis=0, keepdims=True)


def to_column(line, rows):
    lane = lax.broadcasted_iota(jnp.int32, (rows, 128), 1)
    row = lax.broadcasted_iota(jnp.int32, (rows, 128), 0)
    return jnp.sum(jnp.where(lane == row, line, 0.0), axis=1, keepdims=True)


def three_products(values, high_ref, low_ref):
    high = values.astype(jnp.bfloat16)
    low = (values - high.astype(f32)).astype(jnp.bfloat16)
    dot = functools.partial(jnp.dot, preferred_element_type=f32)
    return dot(high, high_ref[...]) + (dot(low, high_ref[...]) + dot(high, low_ref[...]))


def conv_kernel(
    members, chans, norm, prod_ref, filt_ref, grad_ref, cos_ref, sin_ref, twist_ref,
    fwd_high, fwd_low, inv_high, inv_low, out_ref,
    turned, packed, tops, got, got_tops, back, back_tops, home, home_tops, waves, spectra,
    send_sem, top_send, recv_sem, top_recv, back_send, back_top_send, back_recv, back_top_recv,
):
    me = lax.axis_index("ctx")
    mine = lax.axis_index("ch")
    rows = prod_ref.shape[0]
    half = members // 2

    def target(other):
        return (other, mine)

    barrier = pltpu.get_barrier_semaphore()

    def greet(step, carry):
        other = lax.rem(me + step, members)
        pl.semaphore_signal(
            barrier, inc=1, device_id=target(other), device_id_type=pl.DeviceIdType.MESH
        )
        return carry

    lax.fori_loop(1, members, greet, 0)

    for which, ref in enumerate((prod_ref, filt_ref, grad_ref)):
        turned[which] = ref[...].T

    def pack(other, carry):
        for which in range(3):
            values = turned[which, pl.ds(pl.multiple_of(other * chans, chans), chans), :]
            top = row_top(values)
            packed[other, which] = encode(values, top)
            tops[other, which : which + 1, :] = to_lanes(top)
        return carry

    lax.fori_loop(0, members, pack, 0)
    pl.semaphore_wait(barrier, members - 1)

    def outward(other, source):
        return (
            pltpu.make_async_remote_copy(
                src_ref=packed.at[other], dst_ref=got.at[source],
                send_sem=send_sem.at[other], recv_sem=recv_sem.at[source],
                device_id=target(other), device_id_type=pl.DeviceIdType.MESH,
            ),
            pltpu.make_async_remote_copy(
                src_ref=tops.at[other], dst_ref=got_tops.at[source],
                send_sem=top_send.at[other], recv_sem=top_recv.at[source],
                device_id=target(other), device_id_type=pl.DeviceIdType.MESH,
            ),
        )

    def homeward(other, source):
        return (
            pltpu.make_async_remote_copy(
                src_ref=back.at[other], dst_ref=home.at[source],
                send_sem=back_send.at[other], recv_sem=back_recv.at[source],
                device_id=target(other), device_id_type=pl.DeviceIdType.MESH,
            ),
            pltpu.make_async_remote_copy(
                src_ref=back_tops.at[other], dst_ref=home_tops.at[source],
                send_sem=back_top_send.at[other], recv_sem=back_top_recv.at[source],
                device_id=target(other), device_id_type=pl.DeviceIdType.MESH,
            ),
        )

    def post(step, carry):
        for copy in outward(lax.rem(me + step, members), me):
            copy.start()
        return carry

    lax.fori_loop(1, members, post, 0)
    got[me] = packed[me]
    got_tops[me] = tops[me]

    def unpack(step, carry):
        source = lax.rem(me + members - step, members)

        @pl.when(step > 0)
        def _():
            for copy in outward(source, source):
                copy.wait_recv()

        for which in range(3):
            top = to_column(got_tops[source, which : which + 1, :], chans)
            if which == 1:
                top = top * norm
            waves[which, source] = decode(got[source, which], top)
        return carry

    lax.fori_loop(0, members, unpack, 0)

    def coarse(index, carry):
        which = index // (half + 1)
        freq = lax.rem(index, half + 1)
        sums = []
        for parity in range(2):
            real = jnp.zeros((chans, rows), f32)
            imag = jnp.zeros((chans, rows), f32)
            for block in range(parity, members, 2):
                value = waves[which, block]
                real = real + cos_ref[freq, block] * value
                imag = imag - sin_ref[freq, block] * value
            sums.append((real, imag))
        (er, ei), (odd_r, odd_i) = sums

        def put(place, real, imag):
            cosine = twist_ref[0, pl.ds(place, 1), :]
            sine = twist_ref[1, pl.ds(place, 1), :]
            spectra[which, place, :, :rows] = real * cosine + imag * sine
            spectra[which, place, :, rows:] = imag * cosine - real * sine

        put(members - freq, er - odd_r, odd_i - ei)
        put(freq, er + odd_r, ei + odd_i)
        return carry

    lax.fori_loop(0, 3 * (half + 1), coarse, 0)

    height = (members + 1) * chans

    def fine(which, carry):
        flat = spectra[which].reshape(height, 2 * rows)
        spectra[which] = three_products(flat, fwd_high, fwd_low).reshape(
            members + 1, chans, 2 * rows
        )
        return carry

    lax.fori_loop(0, 3, fine, 0)

    def multiply(freq, carry):
        (pr, pi), (hr, hi), (gr, gi) = [
            (spectra[which, freq, :, :rows], spectra[which, freq, :, rows:]) for which in range(3)
        ]
        spectra[0, freq, :, :rows] = pr * hr - pi * hi
        spectra[0, freq, :, rows:] = pr * hi + pi * hr
        spectra[1, freq, :, :rows] = hr * gr + hi * gi
        spectra[1, freq, :, rows:] = hr * gi - hi * gr
        spectra[2, freq, :, :rows] = pr * gr + pi * gi
        spectra[2, freq, :, rows:] = pr * gi - pi * gr
        return carry

    lax.fori_loop(0, members + 1, multiply, 0)

    def unfine(which, carry):
        flat = spectra[which].reshape(height, 2 * rows)
        spectra[which] = three_products(flat, inv_high, inv_low).reshape(
            members + 1, chans, 2 * rows
        )
        return carry

    lax.fori_loop(0, 3, unfine, 0)

    def untwist(index, carry):
        which = index // (half + 1)
        freq = lax.rem(index, half + 1)

        def turn(place):
            cosine = twist_ref[0, pl.ds(place, 1), :]
            sine = twist_ref[1, pl.ds(place, 1), :]
            real = spectra[which, place, :, :rows]
            imag = spectra[which, place, :, rows:]
            return real * cosine - imag * sine, imag * cosine + real * sine

        lr, li = turn(freq)
        ur, ui = turn(members - freq)
        ones = jnp.where(freq == half, 0.0, 1.0)
        weight = jnp.where(freq == 0, 1.0, 2.0) / (2.0 * members * rows)
        spectra[which, freq, :, :rows] = weight * (lr + ones * ur)
        spectra[which, freq, :, rows:] = weight * (li - ones * ui)

        @pl.when(freq < half)
        def _():
            spectra[which, members - freq, :, :rows] = weight * (lr - ur)
            spectra[which, members - freq, :, rows:] = weight * (li + ui)

        return carry

    lax.fori_loop(0, 3 * (half + 1), untwist, 0)

    def finish(block, odd):
        for which in range(3):
            total = jnp.zeros((chans, rows), f32)
            for freq in range(half + 1):
                place = members - freq if odd else freq
                total = total + cos_ref[freq, block] * spectra[which, place, :, :rows]
                total = total - sin_ref[freq, block] * spectra[which, place, :, rows:]
            if which == 2:
                total = total * norm
            top = row_top(total)
            back[block, which] = encode(total, top)
            back_tops[block, which : which + 1, :] = to_lanes(top)

        @pl.when(block != me)
        def _():
            for copy in homeward(block, me):
                copy.start()

    def finish_pair(pair, carry):
        finish(2 * pair, False)
        finish(2 * pair + 1, True)
        return carry

    lax.fori_loop(0, half, finish_pair, 0)
    home[me] = back[me]
    home_tops[me] = back_tops[me]

    def settle(step, carry):
        source = lax.rem(me + members - step, members)

        @pl.when(step > 0)
        def _():
            for copy in homeward(source, source):
                copy.wait_recv()

        for which in range(3):
            top = to_column(home_tops[source, which : which + 1, :], chans)
            turned[which, pl.ds(pl.multiple_of(source * chans, chans), chans), :] = decode(
                home[source, which], top
            )
        return carry

    lax.fori_loop(0, members, settle, 0)
    for which in range(3):
        out_ref[which] = turned[which].T

    def drain(step, carry):
        other = lax.rem(me + step, members)
        for copy in outward(other, me) + homeward(other, me):
            copy.wait_send()
        return carry

    lax.fori_loop(1, members, drain, 0)


def tables(members, rows):
    period = 2 * members * rows
    coarse = np.outer(np.arange(members // 2 + 1), np.arange(members)) % (2 * members)
    coarse = coarse * (math.pi / members)
    twist = np.outer(np.arange(members + 1), np.arange(rows)) % period * (2.0 * math.pi / period)
    fine = np.outer(np.arange(rows), np.arange(rows)) % rows * (2.0 * math.pi / rows)
    c, s = np.cos(fine), np.sin(fine)
    forward = np.block([[c, -s], [s, c]])

    def split(matrix):
        high = matrix.astype(jnp.bfloat16)
        return high, (matrix - high.astype(np.float64)).astype(jnp.bfloat16)

    return (
        np.cos(coarse).astype(np.float32),
        np.sin(coarse).astype(np.float32),
        np.stack([np.cos(twist), np.sin(twist)]).astype(np.float32),
        *split(forward),
        *split(forward.T),
    )


def convolutions(product, long_filter, grad_long, norm):
    members = lax.axis_size("ctx")
    rows, width = product.shape
    chans = width // members
    vmem = pl.BlockSpec(memory_space=pltpu.VMEM)
    smem = pl.BlockSpec(memory_space=pltpu.SMEM)
    wire = pltpu.VMEM((members, 3, chans, rows), jnp.bfloat16)
    peaks = pltpu.VMEM((members, 8, 128), f32)
    sems = pltpu.SemaphoreType.DMA((members,))
    return pl.pallas_call(
        functools.partial(conv_kernel, members, chans, norm),
        out_shape=jax.ShapeDtypeStruct((3, rows, width), f32),
        in_specs=[vmem] * 3 + [smem] * 2 + [vmem] * 5,
        out_specs=vmem,
        scratch_shapes=[
            pltpu.VMEM((3, width, rows), f32),
            wire, peaks, wire, peaks, wire, peaks, wire, peaks,
            pltpu.VMEM((3, members, chans, rows), f32),
            pltpu.VMEM((3, members + 1, chans, 2 * rows), f32),
        ]
        + [sems] * 8,
        compiler_params=pltpu.CompilerParams(
            collective_id=0, has_side_effects=True, vmem_limit_bytes=48 * 1024 * 1024
        ),
    )(product, long_filter, grad_long, *[jnp.asarray(t) for t in tables(members, rows)])


def on_device(streams, short_weight, long_filter, cotangent):
    kernel_len = short_weight.shape[1]
    block_rows = streams.shape[1]
    norm_factor = 1.0 / math.sqrt(block_rows * lax.axis_size("ctx"))
    previous = passed_along(streams[:, block_rows - (kernel_len - 1) :, :], "ctx", 1)
    extended = jnp.concatenate([previous, streams], axis=1)
    features = jnp.zeros(streams.shape, f32)
    for offset in range(kernel_len):
        start = kernel_len - 1 - offset
        features = (
            features + short_weight[:, offset, None, :] * extended[:, start : start + block_rows, :]
        )
    grad_out = cotangent.astype(f32)
    mixed_long, grad_product, filter_grad = convolutions(
        features[1] * features[2], long_filter, grad_out * features[0], norm_factor
    )
    hyena_out = (features[0] * mixed_long).astype(jnp.bfloat16)
    grad_query = grad_out * mixed_long
    feature_grad = jnp.stack([grad_query, grad_product * features[2], grad_product * features[1]])
    following = passed_along(
        feature_grad[:, : kernel_len - 1, :].astype(jnp.bfloat16), "ctx", -1
    ).astype(f32)
    grad_ext = jnp.concatenate([feature_grad, following], axis=1)
    stream_grad = jnp.zeros(feature_grad.shape, f32)
    short_parts = []
    for offset in range(kernel_len):
        stream_grad = (
            stream_grad
            + short_weight[:, offset, None, :] * grad_ext[:, offset : offset + block_rows, :]
        )
        start = kernel_len - 1 - offset
        short_parts.append(
            jnp.sum(feature_grad * extended[:, start : start + block_rows, :], axis=1)
        )
    short_grad = lax.psum(jnp.stack(short_parts, axis=1), "ctx")
    return (hyena_out, stream_grad.astype(jnp.bfloat16), short_grad, filter_grad)


def solution(mesh):
    placed = (P(None, "ctx", "ch"), P(None, None, "ch"), P("ctx", "ch"), P("ctx", "ch"))
    return jax.shard_map(
        on_device,
        mesh=mesh,
        in_specs=placed,
        out_specs=(P("ctx", "ch"), P(None, "ctx", "ch"), P(None, None, "ch"), P("ctx", "ch")),
        check_vma=False,
    )
```

```python
import functools
import math

import jax
import jax.numpy as jnp
import numpy as np
from jax import lax
from jax.experimental import pallas as pl
from jax.experimental.pallas import tpu as pltpu
from jax.sharding import PartitionSpec as P

span = 250.0
half_span = 125.0
tiny = 1e-30
edge = 8
step_rows = 32
f32 = jnp.float32


def encode(values, top):
    power = jnp.abs(values) * (span / top) - half_span
    code = jnp.exp2(power)
    return jnp.where(values < 0.0, -code, code).astype(jnp.bfloat16)


def decode(code, top):
    code = code.astype(f32)
    size = (jnp.log2(jnp.abs(code)) + half_span) * (top * (1.0 / span))
    return jnp.where(code < 0.0, -size, size)


def row_top(values):
    return jnp.maximum(jnp.max(jnp.abs(values), axis=1, keepdims=True), tiny)


def to_lanes(column):
    rows = column.shape[0]
    lane = lax.broadcasted_iota(jnp.int32, (rows, 128), 1)
    row = lax.broadcasted_iota(jnp.int32, (rows, 128), 0)
    return jnp.sum(jnp.where(lane == row, column, 0.0), axis=0, keepdims=True)


def to_column(line, rows):
    lane = lax.broadcasted_iota(jnp.int32, (rows, 128), 1)
    row = lax.broadcasted_iota(jnp.int32, (rows, 128), 0)
    return jnp.sum(jnp.where(lane == row, line, 0.0), axis=1, keepdims=True)


def three_products(values, high_ref, low_ref):
    high = values.astype(jnp.bfloat16)
    low = (values - high.astype(f32)).astype(jnp.bfloat16)
    dot = functools.partial(jnp.dot, preferred_element_type=f32)
    return dot(high, high_ref[...]) + (dot(low, high_ref[...]) + dot(high, low_ref[...]))


def feature_rows(extended_ref, weight_ref, which, start):
    taps = weight_ref.shape[1]
    window = extended_ref[which, pl.ds(start, step_rows + edge), :]
    total = weight_ref[which, 0:1, :] * window[edge : edge + step_rows]
    for tap in range(1, taps):
        total = total + weight_ref[which, tap : tap + 1, :] * window[edge - tap : edge - tap + step_rows]
    return total


def hyena_kernel(
    members, norm, streams_ref, weight_ref, filt_ref, cot_ref, cos_ref, sin_ref, twist_ref,
    fwd_high, fwd_low, inv_high, inv_low,
    hyena_ref, stream_grad_ref, short_ref, filter_grad_ref,
    turned, packed, tops, got, got_tops, back, back_tops, last_tops, home, home_tops, home_last,
    waves, spectra, work, features, extended, grads, halo, edge_out, edge_in, parts, gathered, sums,
    send_sem, recv_sem, top_send, top_recv, back_send, back_recv, back_top_send, back_top_recv,
    last_send, last_recv, halo_sem, edge_sem, part_send, part_recv, sum_send, sum_recv,
):
    me = lax.axis_index("ctx")
    mine = lax.axis_index("ch")
    rows, width = filt_ref.shape
    chans = width // members
    half = members // 2
    taps = weight_ref.shape[1]
    lane_tiles = width // 128
    pieces = 3 * lane_tiles
    chunks = rows // step_rows

    def remote(source, target, sent, received, other):
        return pltpu.make_async_remote_copy(
            src_ref=source, dst_ref=target, send_sem=sent, recv_sem=received,
            device_id=(other, mine), device_id_type=pl.DeviceIdType.MESH,
        )

    def others(body):
        def one(step, carry):
            body(lax.rem(me + step, members))
            return carry

        lax.fori_loop(1, members, one, 0)

    def outward(which, other, source):
        return remote(
            packed.at[which, other], got.at[which, source],
            send_sem.at[which], recv_sem.at[which], other,
        )

    def outward_top(other, source):
        return remote(
            tops.at[other], got_tops.at[source], top_send.at[0], top_recv.at[0], other
        )

    def homeward(which, other, source):
        return remote(
            back.at[which, other], home.at[which, source],
            back_send.at[which], back_recv.at[which], other,
        )

    def homeward_top(other, source):
        return remote(
            back_tops.at[other], home_tops.at[source],
            back_top_send.at[0], back_top_recv.at[0], other,
        )

    def homeward_last(other, source):
        return remote(
            last_tops.at[other], home_last.at[source],
            last_send.at[0], last_recv.at[0], other,
        )

    def part_out(piece, source):
        return remote(
            parts.at[piece], gathered.at[source], part_send.at[piece], part_recv.at[0], piece
        )

    def sum_out(other, piece):
        return remote(
            sums.at[piece], sums.at[piece], sum_send.at[0], sum_recv.at[piece], other
        )

    most = pl.ds(0, members - 1)
    near = lax.rem(me + 1, members)

    def outward_all(which):
        return remote(
            packed.at[which, most], got.at[which, most], send_sem.at[which], recv_sem.at[which], near
        )

    def homeward_all(which):
        return remote(
            back.at[which, most], home.at[which, most], back_send.at[which], back_recv.at[which], near
        )

    outward_top_all = remote(
        tops.at[most], got_tops.at[most], top_send.at[0], top_recv.at[0], near
    )
    homeward_top_all = remote(
        back_tops.at[most], home_tops.at[most], back_top_send.at[0], back_top_recv.at[0], near
    )
    homeward_last_all = remote(
        last_tops.at[most], home_last.at[most], last_send.at[0], last_recv.at[0], near
    )
    part_all = remote(
        gathered.at[most], gathered.at[most], sum_send.at[0], part_recv.at[0], near
    )
    sum_all = remote(
        gathered.at[most], gathered.at[most], sum_send.at[0], part_recv.at[0], near
    )

    barrier = pltpu.get_barrier_semaphore()

    def greet(other):
        pl.semaphore_signal(
            barrier, inc=1, device_id=(other, mine), device_id_type=pl.DeviceIdType.MESH
        )

    others(greet)

    def pack(which, other):
        values = turned[which, other * chans : other * chans + chans, :]
        top = row_top(values)
        packed[which, other] = encode(values, top)
        tops[other, :, which * 128 : which * 128 + 128] = to_lanes(top)

    def pack_all(which):
        for other in range(members):
            pack(which, other)

    halo_out = remote(
        streams_ref.at[:, pl.ds(rows - 16, 16), :], halo, halo_sem.at[0], halo_sem.at[1],
        lax.rem(me + 1, members),
    )
    turned[0] = filt_ref[...].T
    pack_all(0)
    pl.semaphore_wait(barrier, members - 1)

    @pl.when(me < members - 1)
    def _():
        halo_out.start()

    others(lambda other: outward(0, other, me).start())
    got[0, me] = packed[0, me]

    for which in range(3):
        extended[which, edge:, :] = streams_ref[which].astype(f32)

    @pl.when(me > 0)
    def _():
        halo_out.wait_recv()
        for which in range(3):
            extended[which, :edge, :] = halo[which].astype(f32)[16 - edge :]

    @pl.when(me == 0)
    def _():
        extended[:, :edge, :] = jnp.zeros((3, edge, width), f32)

    def featurize(step, carry):
        start = pl.multiple_of(step * step_rows, step_rows)
        query, key, value = [
            feature_rows(extended, weight_ref, which, start) for which in range(3)
        ]
        here = pl.ds(start, step_rows)
        features[0, here, :] = query
        features[1, here, :] = key
        features[2, here, :] = value
        grads[0, here, :] = key * value
        grads[1, here, :] = cot_ref[here, :].astype(f32) * query
        return carry

    lax.fori_loop(0, chunks, featurize, 0)
    turned[1] = grads[0, :rows, :].T
    turned[2] = grads[1, :rows, :].T
    pack_all(1)
    pack_all(2)
    others(lambda other: outward_top(other, me).start())
    others(lambda other: outward(1, other, me).start())
    others(lambda other: outward(2, other, me).start())
    got[1, me] = packed[1, me]
    got[2, me] = packed[2, me]
    got_tops[me] = tops[me]
    outward_top_all.wait_recv()

    height = (members + 1) * chans

    def forward(which):
        outward_all(which).wait_recv()
        for source in range(members):
            top = to_column(got_tops[source, :, which * 128 : which * 128 + 128], chans)
            if which == 0:
                top = top * norm
            waves[source] = decode(got[which, source], top)

        def coarse(freq, carry):
            sides = []
            for parity in range(2):
                real = jnp.zeros((chans, rows), f32)
                imag = jnp.zeros((chans, rows), f32)
                for block in range(parity, members, 2):
                    value = waves[block]
                    real = real + cos_ref[freq, block] * value
                    imag = imag - sin_ref[freq, block] * value
                sides.append((real, imag))
            (even_r, even_i), (odd_r, odd_i) = sides

            def put(place, real, imag):
                cosine = twist_ref[0, pl.ds(place, 1), :]
                sine = twist_ref[1, pl.ds(place, 1), :]
                spectra[which, place, :, :rows] = real * cosine + imag * sine
                spectra[which, place, :, rows:] = imag * cosine - real * sine

            put(members - freq, even_r - odd_r, odd_i - even_i)
            put(freq, even_r + odd_r, even_i + odd_i)
            return carry

        lax.fori_loop(0, half + 1, coarse, 0)
        flat = spectra[which].reshape(height, 2 * rows)
        spectra[which] = three_products(flat, fwd_high, fwd_low).reshape(
            members + 1, chans, 2 * rows
        )

    def inverse(which, left, right, sign):
        def multiply(freq, carry):
            lr, li = spectra[left, freq, :, :rows], spectra[left, freq, :, rows:] * sign
            rr, ri = spectra[right, freq, :, :rows], spectra[right, freq, :, rows:]
            work[freq, :, :rows] = lr * rr - li * ri
            work[freq, :, rows:] = lr * ri + li * rr
            return carry

        lax.fori_loop(0, members + 1, multiply, 0)
        flat = work[...].reshape(height, 2 * rows)
        work[...] = three_products(flat, inv_high, inv_low).reshape(members + 1, chans, 2 * rows)

        def untwist(freq, carry):
            def turn(place):
                cosine = twist_ref[0, pl.ds(place, 1), :]
                sine = twist_ref[1, pl.ds(place, 1), :]
                real = work[place, :, :rows]
                imag = work[place, :, rows:]
                return real * cosine - imag * sine, imag * cosine + real * sine

            lr, li = turn(freq)
            ur, ui = turn(members - freq)
            ones = jnp.where(freq == half, 0.0, 1.0)
            weight = jnp.where(freq == 0, 1.0, 2.0) * (scale / (2.0 * members * rows))
            work[freq, :, :rows] = weight * (lr + ones * ur)
            work[freq, :, rows:] = weight * (li - ones * ui)

            @pl.when(freq < half)
            def _():
                work[members - freq, :, :rows] = weight * (lr - ur)
                work[members - freq, :, rows:] = weight * (li + ui)

            return carry

        scale = norm if which == 2 else 1.0
        lax.fori_loop(0, half + 1, untwist, 0)

        def total_of(block, odd):
            total = jnp.zeros((chans, rows), f32)
            for freq in range(half + 1):
                place = members - freq if odd else freq
                total = total + cos_ref[freq, block] * work[place, :, :rows]
                total = total - sin_ref[freq, block] * work[place, :, rows:]
            return total

        def finish(step, carry):
            blocks = [step * 4 + place for place in range(4)]
            totals = [total_of(block, place % 2 == 1) for place, block in enumerate(blocks)]
            for block, total in zip(blocks, totals):
                top = row_top(total)
                back[which, block] = encode(total, top)
                if which < 2:
                    back_tops[block, :, which * 128 : which * 128 + 128] = to_lanes(top)
                else:
                    last_tops[block] = to_lanes(top)
            for block in blocks:

                @pl.when(block != me)
                def _():
                    homeward(which, block, me).start()
                    if which == 1:
                        homeward_top(block, me).start()
                    if which == 2:
                        homeward_last(block, me).start()

            return carry

        lax.fori_loop(0, members // 4, finish, 0)
        home[which, me] = back[which, me]
        if which == 1:
            home_tops[me] = back_tops[me]
        if which == 2:
            home_last[me] = last_tops[me]

    forward(0)
    forward(1)
    inverse(0, 0, 1, 1.0)
    forward(2)
    inverse(1, 0, 2, -1.0)
    inverse(2, 1, 2, -1.0)

    def settle(which):
        homeward_all(which).wait_recv()
        if which == 2:
            homeward_last_all.wait_recv()
        for source in range(members):
            if which < 2:
                line = home_tops[source, :, which * 128 : which * 128 + 128]
            else:
                line = home_last[source]
            turned[which, source * chans : source * chans + chans, :] = decode(
                home[which, source], to_column(line, chans)
            )

    homeward_top_all.wait_recv()
    settle(0)
    settle(1)
    grads[0, :rows, :] = turned[0].T
    grads[1, :rows, :] = turned[1].T

    def gate(step, carry):
        start = pl.multiple_of(step * step_rows, step_rows)
        here = pl.ds(start, step_rows)
        mixed = grads[0, here, :]
        grad_product = grads[1, here, :]
        hyena_ref[here, :] = (features[0, here, :] * mixed).astype(jnp.bfloat16)
        grads[0, here, :] = cot_ref[here, :].astype(f32) * mixed
        grads[1, here, :] = grad_product * features[2, here, :]
        grads[2, here, :] = grad_product * features[1, here, :]
        return carry

    gate(0, 0)
    edge_out[...] = grads[:, :edge, :]
    edge_copy = remote(
        edge_out, edge_in, edge_sem.at[0], edge_sem.at[1], lax.rem(me + members - 1, members)
    )

    @pl.when(me > 0)
    def _():
        edge_copy.start()

    lax.fori_loop(1, chunks, gate, 0)

    for which in range(3):

        def tap_sums(step, carry):
            start = pl.multiple_of(step * step_rows, step_rows)
            window = extended[which, pl.ds(start, step_rows + edge), :]
            grad = grads[which, pl.ds(start, step_rows), :]
            return tuple(
                total
                + jnp.sum(
                    (grad * window[edge - tap : edge - tap + step_rows]).reshape(
                        step_rows // 8, 8, width
                    ),
                    axis=0,
                )
                for tap, total in enumerate(carry)
            )

        totals = lax.fori_loop(
            0, chunks, tap_sums, tuple(jnp.zeros((8, width), f32) for _ in range(taps))
        )
        lines = [jnp.sum(total, axis=0, keepdims=True) for total in totals]
        lines.append(jnp.zeros((8 - taps, width), f32))
        block = jnp.concatenate(lines, axis=0)
        for tile in range(lane_tiles):
            parts[which * lane_tiles + tile] = block[:, tile * 128 : tile * 128 + 128]

    def each_piece(body):
        def one(piece, carry):
            @pl.when(piece != me)
            def _():
                body(piece)

            return carry

        lax.fori_loop(0, pieces, one, 0)

    each_piece(lambda piece: part_out(piece, me).start())

    @pl.when(me < members - 1)
    def _():
        edge_copy.wait_recv()
        grads[:, rows:, :] = edge_in[...]

    @pl.when(me == members - 1)
    def _():
        grads[:, rows:, :] = jnp.zeros((3, edge, width), f32)

    def back_taps(step, carry):
        start = pl.multiple_of(step * step_rows, step_rows)
        for which in range(3):
            window = grads[which, pl.ds(start, step_rows + edge), :]
            total = weight_ref[which, 0:1, :] * window[:step_rows]
            for tap in range(1, taps):
                total = total + weight_ref[which, tap : tap + 1, :] * window[tap : tap + step_rows]
            stream_grad_ref[which, pl.ds(start, step_rows), :] = total.astype(jnp.bfloat16)
        return carry

    lax.fori_loop(0, chunks, back_taps, 0)

    @pl.when(me < pieces)
    def _():
        gathered[me] = parts[me]
        part_all.wait_recv()
        total = gathered[0]
        for source in range(1, members):
            total = total + gathered[source]
        sums[me] = total
        others(lambda other: sum_out(other, me).start())

    settle(2)
    filter_grad_ref[...] = turned[2].T

    each_piece(lambda piece: sum_out(piece, piece).wait_recv())
    for which in range(3):
        for tile in range(lane_tiles):
            short_ref[which, :, tile * 128 : tile * 128 + 128] = sums[which * lane_tiles + tile][
                :taps
            ]

    for which in range(3):
        outward_all(which).wait_send()
        homeward_all(which).wait_send()
    outward_top_all.wait_send()
    homeward_top_all.wait_send()
    homeward_last_all.wait_send()
    each_piece(lambda piece: part_out(piece, me).wait_send())

    @pl.when(me < pieces)
    def _():
        sum_all.wait_send()

    @pl.when(me < members - 1)
    def _():
        halo_out.wait_send()

    @pl.when(me > 0)
    def _():
        edge_copy.wait_send()


def tables(members, rows):
    period = 2 * members * rows
    coarse = np.outer(np.arange(members // 2 + 1), np.arange(members)) % (2 * members)
    coarse = coarse * (math.pi / members)
    twist = np.outer(np.arange(members + 1), np.arange(rows)) % period * (2.0 * math.pi / period)
    fine = np.outer(np.arange(rows), np.arange(rows)) % rows * (2.0 * math.pi / rows)
    c, s = np.cos(fine), np.sin(fine)
    forward = np.block([[c, -s], [s, c]])

    def split(matrix):
        high = matrix.astype(jnp.bfloat16)
        return high, (matrix - high.astype(np.float64)).astype(jnp.bfloat16)

    return (
        np.cos(coarse).astype(np.float32),
        np.sin(coarse).astype(np.float32),
        np.stack([np.cos(twist), np.sin(twist)]).astype(np.float32),
        *split(forward),
        *split(forward.T),
    )


def hand_over(*refs):
    sem = refs[8]
    copies = [
        pltpu.make_async_copy(source, target, sem.at[place])
        for place, (source, target) in enumerate(zip(refs[:4], refs[4:8]))
    ]
    for copy in copies:
        copy.start()
    for copy in copies:
        copy.wait()


def on_device(streams, short_weight, long_filter, cotangent):
    members = lax.axis_size("ctx")
    rows, width = long_filter.shape
    chans = width // members
    pieces = 3 * (width // 128)
    norm = 1.0 / math.sqrt(rows * members)
    vmem = pl.BlockSpec(memory_space=pltpu.VMEM)
    smem = pl.BlockSpec(memory_space=pltpu.SMEM)
    wire = pltpu.VMEM((3, members, chans, rows), jnp.bfloat16)
    dma = pltpu.SemaphoreType.DMA
    results = tuple(
        pl.pallas_call(
            functools.partial(hyena_kernel, members, norm),
            out_shape=(
                jax.ShapeDtypeStruct((rows, width), jnp.bfloat16),
                jax.ShapeDtypeStruct(streams.shape, jnp.bfloat16),
                jax.ShapeDtypeStruct(short_weight.shape, f32),
                jax.ShapeDtypeStruct((rows, width), f32),
            ),
            in_specs=[vmem] * 4 + [smem] * 2 + [vmem] * 5,
            out_specs=(vmem,) * 4,
            scratch_shapes=[
                pltpu.VMEM((3, width, rows), f32),
                wire,
                pltpu.VMEM((members, 1, 384), f32),
                wire,
                pltpu.VMEM((members, 1, 384), f32),
                wire,
                pltpu.VMEM((members, 1, 256), f32),
                pltpu.VMEM((members, 1, 128), f32),
                wire,
                pltpu.VMEM((members, 1, 256), f32),
                pltpu.VMEM((members, 1, 128), f32),
                pltpu.VMEM((members, chans, rows), f32),
                pltpu.VMEM((3, members + 1, chans, 2 * rows), f32),
                pltpu.VMEM((members + 1, chans, 2 * rows), f32),
                pltpu.VMEM((3, rows, width), f32),
                pltpu.VMEM((3, rows + edge, width), f32),
                pltpu.VMEM((3, rows + edge, width), f32),
                pltpu.VMEM((3, 16, width), jnp.bfloat16),
                pltpu.VMEM((3, edge, width), f32),
                pltpu.VMEM((3, edge, width), f32),
                pltpu.VMEM((pieces, 8, 128), f32),
                pltpu.VMEM((members, 8, 128), f32),
                pltpu.VMEM((pieces, 8, 128), f32),
                dma((3,)),
                dma((3,)),
                dma((1,)),
                dma((1,)),
                dma((3,)),
                dma((3,)),
                dma((1,)),
                dma((1,)),
                dma((1,)),
                dma((1,)),
                dma((2,)),
                dma((2,)),
                dma((pieces,)),
                dma((1,)),
                dma((1,)),
                dma((pieces,)),
            ],
            compiler_params=pltpu.CompilerParams(
                collective_id=0, has_side_effects=True, vmem_limit_bytes=56 * 1024 * 1024
            ),
        )(
            streams, short_weight, long_filter, cotangent,
            *[jnp.asarray(t) for t in tables(members, rows)],
        )
    )
    anywhere = pl.BlockSpec(memory_space=pl.ANY)
    return tuple(
        pl.pallas_call(
            hand_over,
            out_shape=tuple(jax.ShapeDtypeStruct(r.shape, r.dtype) for r in results),
            in_specs=[anywhere] * 4,
            out_specs=(anywhere,) * 4,
            scratch_shapes=[dma((4,))],
            compiler_params=pltpu.CompilerParams(vmem_limit_bytes=60 * 1024 * 1024),
        )(*results)
    )


def solution(mesh):
    placed = (P(None, "ctx", "ch"), P(None, None, "ch"), P("ctx", "ch"), P("ctx", "ch"))
    return jax.shard_map(
        on_device,
        mesh=mesh,
        in_specs=placed,
        out_specs=(P("ctx", "ch"), P(None, "ctx", "ch"), P(None, None, "ch"), P("ctx", "ch")),
        check_vma=False,
    )
```

```python
import functools
import math

import jax
import jax.numpy as jnp
import numpy as np
from jax import lax
from jax.experimental import pallas as pl
from jax.experimental.pallas import tpu as pltpu
from jax.sharding import PartitionSpec as P

span = 250.0
half_span = 125.0
tiny = 1e-30
edge = 8
step_rows = 32
f32 = jnp.float32


def encode(values, top):
    power = jnp.abs(values) * (span / top) - half_span
    code = jnp.exp2(power)
    return jnp.where(values < 0.0, -code, code).astype(jnp.bfloat16)


def decode(code, top):
    code = code.astype(f32)
    size = (jnp.log2(jnp.abs(code)) + half_span) * (top * (1.0 / span))
    return jnp.where(code < 0.0, -size, size)


def row_top(values):
    return jnp.maximum(jnp.max(jnp.abs(values), axis=1, keepdims=True), tiny)


def to_lanes(column):
    rows = column.shape[0]
    lane = lax.broadcasted_iota(jnp.int32, (rows, 128), 1)
    row = lax.broadcasted_iota(jnp.int32, (rows, 128), 0)
    return jnp.sum(jnp.where(lane == row, column, 0.0), axis=0, keepdims=True)


def to_column(line, rows):
    lane = lax.broadcasted_iota(jnp.int32, (rows, 128), 1)
    row = lax.broadcasted_iota(jnp.int32, (rows, 128), 0)
    return jnp.sum(jnp.where(lane == row, line, 0.0), axis=1, keepdims=True)


def three_products(values, table_ref):
    high = values.astype(jnp.bfloat16)
    low = (values - high.astype(f32)).astype(jnp.bfloat16)
    return jnp.dot(
        jnp.concatenate([high, low, high], axis=1), table_ref[...], preferred_element_type=f32
    )


def feature_rows(extended_ref, weight_ref, which, start):
    taps = weight_ref.shape[1]
    window = extended_ref[which, pl.ds(start, step_rows + edge), :]
    total = weight_ref[which, 0:1, :] * window[edge : edge + step_rows]
    for tap in range(1, taps):
        total = total + weight_ref[which, tap : tap + 1, :] * window[edge - tap : edge - tap + step_rows]
    return total


def hyena_kernel(
    members, norm, streams_ref, weight_ref, filt_ref, cot_ref, cos_ref, sin_ref, twist_ref,
    fwd_any, inv_any,
    hyena_ref, stream_grad_ref, short_ref, filter_grad_ref,
    turned, packed, tops, got, got_tops, back, back_tops, home, home_tops,
    waves, spectra, work, features, extended, grads, halo, edge_out, edge_in, parts, gathered, sums,
    send_sem, recv_sem, top_send, top_recv, back_send, back_recv, back_top_send, back_top_recv,
    halo_sem, edge_sem, part_send, part_recv, sum_send, sum_recv,
    fwd_ref, inv_ref, table_sem,
):
    me = lax.axis_index("ctx")
    mine = lax.axis_index("ch")
    rows, width = filt_ref.shape
    chans = width // members
    half = members // 2
    taps = weight_ref.shape[1]
    lane_tiles = width // 128
    pieces = 3 * lane_tiles
    chunks = rows // step_rows

    def remote(source, target, sent, received, other):
        return pltpu.make_async_remote_copy(
            src_ref=source, dst_ref=target, send_sem=sent, recv_sem=received,
            device_id=(other, mine), device_id_type=pl.DeviceIdType.MESH,
        )

    def others(body):
        def one(step, carry):
            body(lax.rem(me + step, members))
            return carry

        lax.fori_loop(1, members, one, 0)

    def outward(which, other, source):
        return remote(
            packed.at[which, other], got.at[which, source],
            send_sem.at[which], recv_sem.at[which], other,
        )

    def outward_top(other, source):
        return remote(
            tops.at[other], got_tops.at[source], top_send.at[0], top_recv.at[0], other
        )

    def homeward(which, other, source):
        return remote(
            back.at[which, other], home.at[which, source],
            back_send.at[which], back_recv.at[which], other,
        )

    def homeward_top(which, other, source):
        return remote(
            back_tops.at[which, other], home_tops.at[which, source],
            back_top_send.at[which], back_top_recv.at[which], other,
        )

    def part_out(piece, source):
        return remote(
            parts.at[piece], gathered.at[source], part_send.at[piece], part_recv.at[0], piece
        )

    def sum_out(other, piece):
        return remote(
            sums.at[piece], sums.at[piece], sum_send.at[0], sum_recv.at[piece], other
        )

    most = pl.ds(0, members - 1)
    near = lax.rem(me + 1, members)

    def outward_all(which):
        return remote(
            packed.at[which, most], got.at[which, most], send_sem.at[which], recv_sem.at[which], near
        )

    def homeward_all(which):
        return remote(
            back.at[which, most], home.at[which, most], back_send.at[which], back_recv.at[which], near
        )

    outward_top_all = remote(
        tops.at[most], got_tops.at[most], top_send.at[0], top_recv.at[0], near
    )
    def homeward_top_all(which):
        return remote(
            back_tops.at[which, most], home_tops.at[which, most],
            back_top_send.at[which], back_top_recv.at[which], near,
        )

    part_all = remote(
        gathered.at[most], gathered.at[most], sum_send.at[0], part_recv.at[0], near
    )
    sum_all = remote(
        gathered.at[most], gathered.at[most], sum_send.at[0], part_recv.at[0], near
    )

    barrier = pltpu.get_barrier_semaphore()

    def greet(other):
        pl.semaphore_signal(
            barrier, inc=1, device_id=(other, mine), device_id_type=pl.DeviceIdType.MESH
        )

    others(greet)
    fwd_copy = pltpu.make_async_copy(fwd_any, fwd_ref, table_sem.at[0])
    inv_copy = pltpu.make_async_copy(inv_any, inv_ref, table_sem.at[1])
    fwd_copy.start()
    inv_copy.start()

    def pack(which, other):
        values = turned[which, other * chans : other * chans + chans, :]
        top = row_top(values)
        packed[which, other] = encode(values, top)
        tops[other, :, which * 128 : which * 128 + 128] = to_lanes(top)

    def pack_all(which):
        for other in range(members):
            pack(which, other)

    halo_out = remote(
        streams_ref.at[:, pl.ds(rows - 16, 16), :], halo, halo_sem.at[0], halo_sem.at[1],
        lax.rem(me + 1, members),
    )
    turned[0] = filt_ref[...].T
    pack_all(0)
    pl.semaphore_wait(barrier, members - 1)

    @pl.when(me < members - 1)
    def _():
        halo_out.start()

    others(lambda other: outward(0, other, me).start())
    got[0, me] = packed[0, me]

    for which in range(3):
        extended[which, edge:, :] = streams_ref[which].astype(f32)

    @pl.when(me > 0)
    def _():
        halo_out.wait_recv()
        for which in range(3):
            extended[which, :edge, :] = halo[which].astype(f32)[16 - edge :]

    @pl.when(me == 0)
    def _():
        extended[:, :edge, :] = jnp.zeros((3, edge, width), f32)

    def featurize(step, carry):
        start = pl.multiple_of(step * step_rows, step_rows)
        query, key, value = [
            feature_rows(extended, weight_ref, which, start) for which in range(3)
        ]
        here = pl.ds(start, step_rows)
        features[0, here, :] = query
        features[1, here, :] = key
        features[2, here, :] = value
        grads[0, here, :] = key * value
        grads[1, here, :] = cot_ref[here, :].astype(f32) * query
        return carry

    lax.fori_loop(0, chunks, featurize, 0)
    turned[1] = grads[0, :rows, :].T
    turned[2] = grads[1, :rows, :].T
    pack_all(1)
    pack_all(2)
    others(lambda other: outward_top(other, me).start())
    others(lambda other: outward(1, other, me).start())
    others(lambda other: outward(2, other, me).start())
    got[1, me] = packed[1, me]
    got[2, me] = packed[2, me]
    got_tops[me] = tops[me]
    outward_top_all.wait_recv()

    height = (members + 1) * chans

    def forward(which):
        outward_all(which).wait_recv()
        for source in range(members):
            top = to_column(got_tops[source, :, which * 128 : which * 128 + 128], chans)
            if which == 0:
                top = top * norm
            waves[source] = decode(got[which, source], top)

        def coarse(freq, carry):
            sides = []
            for parity in range(2):
                real = jnp.zeros((chans, rows), f32)
                imag = jnp.zeros((chans, rows), f32)
                for block in range(parity, members, 2):
                    value = waves[block]
                    real = real + cos_ref[freq, block] * value
                    imag = imag - sin_ref[freq, block] * value
                sides.append((real, imag))
            (even_r, even_i), (odd_r, odd_i) = sides

            def put(place, real, imag):
                cosine = twist_ref[0, pl.ds(place, 1), :]
                sine = twist_ref[1, pl.ds(place, 1), :]
                spectra[which, place, :, :rows] = real * cosine + imag * sine
                spectra[which, place, :, rows:] = imag * cosine - real * sine

            put(members - freq, even_r - odd_r, odd_i - even_i)
            put(freq, even_r + odd_r, even_i + odd_i)
            return carry

        lax.fori_loop(0, half + 1, coarse, 0)
        flat = spectra[which].reshape(height, 2 * rows)
        spectra[which] = three_products(flat, fwd_ref).reshape(
            members + 1, chans, 2 * rows
        )

    def inverse(which, left, right, sign):
        def multiply(freq, carry):
            lr, li = spectra[left, freq, :, :rows], spectra[left, freq, :, rows:] * sign
            rr, ri = spectra[right, freq, :, :rows], spectra[right, freq, :, rows:]
            work[freq, :, :rows] = lr * rr - li * ri
            work[freq, :, rows:] = lr * ri + li * rr
            return carry

        lax.fori_loop(0, members + 1, multiply, 0)
        flat = work[...].reshape(height, 2 * rows)
        work[...] = three_products(flat, inv_ref).reshape(members + 1, chans, 2 * rows)

        def untwist(freq, carry):
            def turn(place):
                cosine = twist_ref[0, pl.ds(place, 1), :]
                sine = twist_ref[1, pl.ds(place, 1), :]
                real = work[place, :, :rows]
                imag = work[place, :, rows:]
                return real * cosine - imag * sine, imag * cosine + real * sine

            lr, li = turn(freq)
            ur, ui = turn(members - freq)
            ones = jnp.where(freq == half, 0.0, 1.0)
            weight = jnp.where(freq == 0, 1.0, 2.0) * (scale / (2.0 * members * rows))
            work[freq, :, :rows] = weight * (lr + ones * ur)
            work[freq, :, rows:] = weight * (li - ones * ui)

            @pl.when(freq < half)
            def _():
                work[members - freq, :, :rows] = weight * (lr - ur)
                work[members - freq, :, rows:] = weight * (li + ui)

            return carry

        scale = norm if which == 2 else 1.0
        lax.fori_loop(0, half + 1, untwist, 0)

        def total_of(block, odd):
            total = jnp.zeros((chans, rows), f32)
            for freq in range(half + 1):
                place = members - freq if odd else freq
                total = total + cos_ref[freq, block] * work[place, :, :rows]
                total = total - sin_ref[freq, block] * work[place, :, rows:]
            return total

        def finish(step, carry):
            blocks = [step * 4 + place for place in range(4)]
            totals = [total_of(block, place % 2 == 1) for place, block in enumerate(blocks)]
            for block, total in zip(blocks, totals):
                top = row_top(total)
                back[which, block] = encode(total, top)
                back_tops[which, block] = to_lanes(top)
            for block in blocks:

                @pl.when(block != me)
                def _():
                    homeward(which, block, me).start()
                    homeward_top(which, block, me).start()

            return carry

        lax.fori_loop(0, members // 4, finish, 0)
        home[which, me] = back[which, me]
        home_tops[which, me] = back_tops[which, me]

    fwd_copy.wait()
    forward(0)
    forward(1)
    inv_copy.wait()
    inverse(0, 0, 1, 1.0)
    forward(2)
    inverse(1, 0, 2, -1.0)
    inverse(2, 1, 2, -1.0)

    def settle(which):
        homeward_top_all(which).wait_recv()
        homeward_all(which).wait_recv()
        for source in range(members):
            turned[which, source * chans : source * chans + chans, :] = decode(
                home[which, source], to_column(home_tops[which, source], chans)
            )

    before = lax.rem(me + members - 1, members)
    query_edge = remote(
        edge_out.at[0], edge_in.at[0], edge_sem.at[0], edge_sem.at[1], before
    )
    other_edges = remote(
        edge_out.at[pl.ds(1, 2)], edge_in.at[pl.ds(1, 2)], edge_sem.at[2], edge_sem.at[3], before
    )

    def gate_query(step, carry):
        here = pl.ds(pl.multiple_of(step * step_rows, step_rows), step_rows)
        mixed = grads[0, here, :]
        hyena_ref[here, :] = (features[0, here, :] * mixed).astype(jnp.bfloat16)
        grads[0, here, :] = cot_ref[here, :].astype(f32) * mixed
        return carry

    def gate_others(step, carry):
        here = pl.ds(pl.multiple_of(step * step_rows, step_rows), step_rows)
        grad_product = grads[1, here, :]
        grads[1, here, :] = grad_product * features[2, here, :]
        grads[2, here, :] = grad_product * features[1, here, :]
        return carry

    def all_taps(which):
        def tap_sums(step, carry):
            start = pl.multiple_of(step * step_rows, step_rows)
            window = extended[which, pl.ds(start, step_rows + edge), :]
            grad = grads[which, pl.ds(start, step_rows), :]
            return tuple(
                total
                + jnp.sum(
                    (grad * window[edge - tap : edge - tap + step_rows]).reshape(
                        step_rows // 8, 8, width
                    ),
                    axis=0,
                )
                for tap, total in enumerate(carry)
            )

        totals = lax.fori_loop(
            0, chunks, tap_sums, tuple(jnp.zeros((8, width), f32) for _ in range(taps))
        )
        lines = [jnp.sum(total, axis=0, keepdims=True) for total in totals]
        lines.append(jnp.zeros((8 - taps, width), f32))
        block = jnp.concatenate(lines, axis=0)
        for tile in range(lane_tiles):
            parts[which * lane_tiles + tile] = block[:, tile * 128 : tile * 128 + 128]

    settle(0)
    grads[0, :rows, :] = turned[0].T
    lax.fori_loop(0, chunks, gate_query, 0)
    edge_out[0] = grads[0, :edge, :]

    @pl.when(me > 0)
    def _():
        query_edge.start()

    all_taps(0)
    settle(1)
    grads[1, :rows, :] = turned[1].T
    lax.fori_loop(0, chunks, gate_others, 0)
    edge_out[1:] = grads[1:, :edge, :]

    @pl.when(me > 0)
    def _():
        other_edges.start()

    all_taps(1)
    all_taps(2)

    def each_piece(body):
        def one(piece, carry):
            @pl.when(piece != me)
            def _():
                body(piece)

            return carry

        lax.fori_loop(0, pieces, one, 0)

    each_piece(lambda piece: part_out(piece, me).start())

    @pl.when(me < members - 1)
    def _():
        query_edge.wait_recv()
        other_edges.wait_recv()
        grads[:, rows:, :] = edge_in[...]

    @pl.when(me == members - 1)
    def _():
        grads[:, rows:, :] = jnp.zeros((3, edge, width), f32)

    def back_taps(step, carry):
        start = pl.multiple_of(step * step_rows, step_rows)
        for which in range(3):
            window = grads[which, pl.ds(start, step_rows + edge), :]
            total = weight_ref[which, 0:1, :] * window[:step_rows]
            for tap in range(1, taps):
                total = total + weight_ref[which, tap : tap + 1, :] * window[tap : tap + step_rows]
            stream_grad_ref[which, pl.ds(start, step_rows), :] = total.astype(jnp.bfloat16)
        return carry

    lax.fori_loop(0, chunks, back_taps, 0)

    @pl.when(me < pieces)
    def _():
        gathered[me] = parts[me]
        part_all.wait_recv()
        total = gathered[0]
        for source in range(1, members):
            total = total + gathered[source]
        sums[me] = total
        others(lambda other: sum_out(other, me).start())

    settle(2)
    filter_grad_ref[...] = turned[2].T

    each_piece(lambda piece: sum_out(piece, piece).wait_recv())
    for which in range(3):
        for tile in range(lane_tiles):
            short_ref[which, :, tile * 128 : tile * 128 + 128] = sums[which * lane_tiles + tile][
                :taps
            ]

    for which in range(3):
        outward_all(which).wait_send()
        homeward_all(which).wait_send()
        homeward_top_all(which).wait_send()
    outward_top_all.wait_send()
    each_piece(lambda piece: part_out(piece, me).wait_send())

    @pl.when(me < pieces)
    def _():
        sum_all.wait_send()

    @pl.when(me < members - 1)
    def _():
        halo_out.wait_send()

    @pl.when(me > 0)
    def _():
        query_edge.wait_send()
        other_edges.wait_send()


def tables(members, rows):
    period = 2 * members * rows
    coarse = np.outer(np.arange(members // 2 + 1), np.arange(members)) % (2 * members)
    coarse = coarse * (math.pi / members)
    twist = np.outer(np.arange(members + 1), np.arange(rows)) % period * (2.0 * math.pi / period)
    fine = np.outer(np.arange(rows), np.arange(rows)) % rows * (2.0 * math.pi / rows)
    c, s = np.cos(fine), np.sin(fine)
    forward = np.block([[c, -s], [s, c]])

    def split(matrix):
        high = matrix.astype(jnp.bfloat16)
        low = (matrix - high.astype(np.float64)).astype(jnp.bfloat16)
        return np.concatenate([high, high, low])

    return (
        np.cos(coarse).astype(np.float32),
        np.sin(coarse).astype(np.float32),
        np.stack([np.cos(twist), np.sin(twist)]).astype(np.float32),
        split(forward),
        split(forward.T),
    )


def hand_over(*refs):
    sem = refs[12]
    arrivals = [
        pltpu.make_async_copy(refs[place], refs[8 + place], sem.at[0, place]) for place in range(4)
    ]
    leaving = [
        pltpu.make_async_copy(refs[8 + place], refs[4 + place], sem.at[1, place])
        for place in range(4)
    ]
    for copy in arrivals:
        copy.start()
    for arrival, copy in zip(arrivals, leaving):
        arrival.wait()
        copy.start()
    for copy in leaving:
        copy.wait()


def on_device(streams, short_weight, long_filter, cotangent):
    members = lax.axis_size("ctx")
    rows, width = long_filter.shape
    chans = width // members
    pieces = 3 * (width // 128)
    norm = 1.0 / math.sqrt(rows * members)
    vmem = pl.BlockSpec(memory_space=pltpu.VMEM)
    smem = pl.BlockSpec(memory_space=pltpu.SMEM)
    wire = pltpu.VMEM((3, members, chans, rows), jnp.bfloat16)
    dma = pltpu.SemaphoreType.DMA
    results = tuple(
        pl.pallas_call(
            functools.partial(hyena_kernel, members, norm),
            out_shape=(
                jax.ShapeDtypeStruct((rows, width), jnp.bfloat16),
                jax.ShapeDtypeStruct(streams.shape, jnp.bfloat16),
                jax.ShapeDtypeStruct(short_weight.shape, f32),
                jax.ShapeDtypeStruct((rows, width), f32),
            ),
            in_specs=[vmem] * 4 + [smem] * 2 + [vmem] + [pl.BlockSpec(memory_space=pl.ANY)] * 2,
            out_specs=(vmem,) * 4,
            scratch_shapes=[
                pltpu.VMEM((3, width, rows), f32),
                wire,
                pltpu.VMEM((members, 1, 384), f32),
                wire,
                pltpu.VMEM((members, 1, 384), f32),
                wire,
                pltpu.VMEM((3, members, 1, 128), f32),
                wire,
                pltpu.VMEM((3, members, 1, 128), f32),
                pltpu.VMEM((members, chans, rows), f32),
                pltpu.VMEM((3, members + 1, chans, 2 * rows), f32),
                pltpu.VMEM((members + 1, chans, 2 * rows), f32),
                pltpu.VMEM((3, rows, width), f32),
                pltpu.VMEM((3, rows + edge, width), f32),
                pltpu.VMEM((3, rows + edge, width), f32),
                pltpu.VMEM((3, 16, width), jnp.bfloat16),
                pltpu.VMEM((3, edge, width), f32),
                pltpu.VMEM((3, edge, width), f32),
                pltpu.VMEM((pieces, 8, 128), f32),
                pltpu.VMEM((members, 8, 128), f32),
                pltpu.VMEM((pieces, 8, 128), f32),
                dma((3,)),
                dma((3,)),
                dma((1,)),
                dma((1,)),
                dma((3,)),
                dma((3,)),
                dma((3,)),
                dma((3,)),
                dma((2,)),
                dma((4,)),
                dma((pieces,)),
                dma((1,)),
                dma((1,)),
                dma((pieces,)),
                pltpu.VMEM((6 * rows, 2 * rows), jnp.bfloat16),
                pltpu.VMEM((6 * rows, 2 * rows), jnp.bfloat16),
                dma((2,)),
            ],
            compiler_params=pltpu.CompilerParams(
                collective_id=0, has_side_effects=True, vmem_limit_bytes=56 * 1024 * 1024
            ),
        )(
            streams, short_weight, long_filter, cotangent,
            *[jnp.asarray(t) for t in tables(members, rows)],
        )
    )
    anywhere = pl.BlockSpec(memory_space=pl.ANY)
    return tuple(
        pl.pallas_call(
            hand_over,
            out_shape=tuple(jax.ShapeDtypeStruct(r.shape, r.dtype) for r in results),
            in_specs=[anywhere] * 4,
            out_specs=(anywhere,) * 4,
            scratch_shapes=[pltpu.VMEM(r.shape, r.dtype) for r in results] + [dma((2, 4))],
            compiler_params=pltpu.CompilerParams(vmem_limit_bytes=60 * 1024 * 1024),
        )(*results)
    )


def solution(mesh):
    placed = (P(None, "ctx", "ch"), P(None, None, "ch"), P("ctx", "ch"), P("ctx", "ch"))
    return jax.shard_map(
        on_device,
        mesh=mesh,
        in_specs=placed,
        out_specs=(P("ctx", "ch"), P(None, "ctx", "ch"), P(None, None, "ch"), P("ctx", "ch")),
        check_vma=False,
    )
```

```python
import functools
import math

import jax
import jax.numpy as jnp
import numpy as np
from jax import lax
from jax.experimental import pallas as pl
from jax.experimental.pallas import tpu as pltpu
from jax.sharding import PartitionSpec as P

span = 250.0
half_span = 125.0
tiny = 1e-30
edge = 8
step_rows = 32
f32 = jnp.float32


def encode(values, top):
    power = jnp.abs(values) * (span / top) - half_span
    code = jnp.exp2(power)
    return jnp.where(values < 0.0, -code, code).astype(jnp.bfloat16)


def decode(code, top):
    code = code.astype(f32)
    size = (jnp.log2(jnp.abs(code)) + half_span) * (top * (1.0 / span))
    return jnp.where(code < 0.0, -size, size)


def row_top(values):
    return jnp.maximum(jnp.max(jnp.abs(values), axis=1, keepdims=True), tiny)


def to_lanes(column):
    rows = column.shape[0]
    lane = lax.broadcasted_iota(jnp.int32, (rows, 128), 1)
    row = lax.broadcasted_iota(jnp.int32, (rows, 128), 0)
    return jnp.sum(jnp.where(lane == row, column, 0.0), axis=0, keepdims=True)


def to_column(line, rows):
    lane = lax.broadcasted_iota(jnp.int32, (rows, 128), 1)
    row = lax.broadcasted_iota(jnp.int32, (rows, 128), 0)
    return jnp.sum(jnp.where(lane == row, line, 0.0), axis=1, keepdims=True)


def three_products(values, table_ref):
    high = values.astype(jnp.bfloat16)
    low = (values - high.astype(f32)).astype(jnp.bfloat16)
    return jnp.dot(
        jnp.concatenate([high, low, high], axis=1), table_ref[...], preferred_element_type=f32
    )


def feature_rows(extended_ref, weight_ref, which, start):
    taps = weight_ref.shape[1]
    window = extended_ref[which, pl.ds(start, step_rows + edge), :]
    total = weight_ref[which, 0:1, :] * window[edge : edge + step_rows]
    for tap in range(1, taps):
        total = total + weight_ref[which, tap : tap + 1, :] * window[edge - tap : edge - tap + step_rows]
    return total


def hyena_kernel(
    members, norm, streams_ref, weight_ref, filt_ref, cot_ref, cos_ref, sin_ref, twist_ref,
    fwd_any, inv_any,
    hyena_ref, stream_grad_ref, short_ref, filter_grad_ref,
    turned, packed, tops, got, got_tops, back, back_tops, home, home_tops,
    waves, spectra, work, features, extended, grads, halo, edge_out, edge_in, parts, gathered, sums,
    send_sem, recv_sem, top_send, top_recv, back_send, back_recv, back_top_send, back_top_recv,
    halo_sem, edge_sem, part_send, part_recv, sum_send, sum_recv,
    fwd_ref, inv_ref, table_sem,
):
    me = lax.axis_index("ctx")
    mine = lax.axis_index("ch")
    rows, width = filt_ref.shape
    chans = width // members
    half = members // 2
    taps = weight_ref.shape[1]
    lane_tiles = width // 128
    pieces = 3 * lane_tiles
    chunks = rows // step_rows

    def remote(source, target, sent, received, other):
        return pltpu.make_async_remote_copy(
            src_ref=source, dst_ref=target, send_sem=sent, recv_sem=received,
            device_id=(other, mine), device_id_type=pl.DeviceIdType.MESH,
        )

    def others(body):
        if members <= 16:
            for step in range(1, members):
                body(lax.rem(me + step, members))
            return

        def one(step, carry):
            body(lax.rem(me + step, members))
            return carry

        lax.fori_loop(1, members, one, 0)

    def outward(which, other, source):
        return remote(
            packed.at[which, other], got.at[which, source],
            send_sem.at[which], recv_sem.at[which], other,
        )

    def outward_top(other, source):
        return remote(
            tops.at[other], got_tops.at[source], top_send.at[0], top_recv.at[0], other
        )

    def homeward(which, other, source):
        return remote(
            back.at[which, other], home.at[which, source],
            back_send.at[which], back_recv.at[which], other,
        )

    def homeward_top(which, other, source):
        return remote(
            back_tops.at[which, other], home_tops.at[which, source],
            back_top_send.at[which], back_top_recv.at[which], other,
        )

    def part_out(piece, source):
        return remote(
            parts.at[piece], gathered.at[source], part_send.at[piece], part_recv.at[0], piece
        )

    def sum_out(other, piece):
        return remote(
            sums.at[piece], sums.at[piece], sum_send.at[0], sum_recv.at[piece], other
        )

    most = pl.ds(0, members - 1)
    near = lax.rem(me + 1, members)

    def outward_all(which):
        return remote(
            packed.at[which, most], got.at[which, most], send_sem.at[which], recv_sem.at[which], near
        )

    def homeward_all(which):
        return remote(
            back.at[which, most], home.at[which, most], back_send.at[which], back_recv.at[which], near
        )

    outward_top_all = remote(
        tops.at[most], got_tops.at[most], top_send.at[0], top_recv.at[0], near
    )
    def homeward_top_all(which):
        return remote(
            back_tops.at[which, most], home_tops.at[which, most],
            back_top_send.at[which], back_top_recv.at[which], near,
        )

    part_all = remote(
        gathered.at[most], gathered.at[most], sum_send.at[0], part_recv.at[0], near
    )
    sum_all = remote(
        gathered.at[most], gathered.at[most], sum_send.at[0], part_recv.at[0], near
    )

    barrier = pltpu.get_barrier_semaphore()

    def greet(other):
        pl.semaphore_signal(
            barrier, inc=1, device_id=(other, mine), device_id_type=pl.DeviceIdType.MESH
        )

    others(greet)
    fwd_copy = pltpu.make_async_copy(fwd_any, fwd_ref, table_sem.at[0])
    inv_copy = pltpu.make_async_copy(inv_any, inv_ref, table_sem.at[1])
    fwd_copy.start()
    inv_copy.start()

    def pack(which, other):
        values = turned[which, other * chans : other * chans + chans, :]
        top = row_top(values)
        packed[which, other] = encode(values, top)
        tops[other, :, which * 128 : which * 128 + 128] = to_lanes(top)

    def pack_all(which):
        for other in range(members):
            pack(which, other)

    halo_out = remote(
        streams_ref.at[:, pl.ds(rows - 16, 16), :], halo, halo_sem.at[0], halo_sem.at[1],
        lax.rem(me + 1, members),
    )
    turned[0] = filt_ref[...].T
    pack_all(0)
    pl.semaphore_wait(barrier, members - 1)

    @pl.when(me < members - 1)
    def _():
        halo_out.start()

    others(lambda other: outward(0, other, me).start())
    got[0, me] = packed[0, me]

    for which in range(3):
        extended[which, edge:, :] = streams_ref[which].astype(f32)

    @pl.when(me > 0)
    def _():
        halo_out.wait_recv()
        for which in range(3):
            extended[which, :edge, :] = halo[which].astype(f32)[16 - edge :]

    @pl.when(me == 0)
    def _():
        extended[:, :edge, :] = jnp.zeros((3, edge, width), f32)

    def featurize(step, carry):
        start = pl.multiple_of(step * step_rows, step_rows)
        query, key, value = [
            feature_rows(extended, weight_ref, which, start) for which in range(3)
        ]
        here = pl.ds(start, step_rows)
        features[0, here, :] = query
        features[1, here, :] = key
        features[2, here, :] = value
        grads[0, here, :] = key * value
        grads[1, here, :] = cot_ref[here, :].astype(f32) * query
        return carry

    lax.fori_loop(0, chunks, featurize, 0)
    turned[2] = grads[1, :rows, :].T
    pack_all(2)
    others(lambda other: outward(2, other, me).start())
    turned[1] = grads[0, :rows, :].T
    pack_all(1)
    others(lambda other: outward_top(other, me).start())
    others(lambda other: outward(1, other, me).start())
    got[1, me] = packed[1, me]
    got[2, me] = packed[2, me]
    got_tops[me] = tops[me]
    outward_top_all.wait_recv()

    height = (members + 1) * chans

    def forward(which):
        outward_all(which).wait_recv()
        for source in range(members):
            top = to_column(got_tops[source, :, which * 128 : which * 128 + 128], chans)
            if which == 0:
                top = top * norm
            waves[source] = decode(got[which, source], top)

        def coarse(freq, carry):
            sides = []
            for parity in range(2):
                real = jnp.zeros((chans, rows), f32)
                imag = jnp.zeros((chans, rows), f32)
                for block in range(parity, members, 2):
                    value = waves[block]
                    real = real + cos_ref[freq, block] * value
                    imag = imag - sin_ref[freq, block] * value
                sides.append((real, imag))
            (even_r, even_i), (odd_r, odd_i) = sides

            def put(place, real, imag):
                cosine = twist_ref[0, pl.ds(place, 1), :]
                sine = twist_ref[1, pl.ds(place, 1), :]
                spectra[which, place, :, :rows] = real * cosine + imag * sine
                spectra[which, place, :, rows:] = imag * cosine - real * sine

            put(members - freq, even_r - odd_r, odd_i - even_i)
            put(freq, even_r + odd_r, even_i + odd_i)
            return carry

        lax.fori_loop(0, half + 1, coarse, 0)
        flat = spectra[which].reshape(height, 2 * rows)
        spectra[which] = three_products(flat, fwd_ref).reshape(
            members + 1, chans, 2 * rows
        )

    def inverse(which, left, right, sign):
        def multiply(freq, carry):
            lr, li = spectra[left, freq, :, :rows], spectra[left, freq, :, rows:] * sign
            rr, ri = spectra[right, freq, :, :rows], spectra[right, freq, :, rows:]
            work[freq, :, :rows] = lr * rr - li * ri
            work[freq, :, rows:] = lr * ri + li * rr
            return carry

        lax.fori_loop(0, members + 1, multiply, 0)
        flat = work[...].reshape(height, 2 * rows)
        work[...] = three_products(flat, inv_ref).reshape(members + 1, chans, 2 * rows)

        def untwist(freq, carry):
            def turn(place):
                cosine = twist_ref[0, pl.ds(place, 1), :]
                sine = twist_ref[1, pl.ds(place, 1), :]
                real = work[place, :, :rows]
                imag = work[place, :, rows:]
                return real * cosine - imag * sine, imag * cosine + real * sine

            lr, li = turn(freq)
            ur, ui = turn(members - freq)
            ones = jnp.where(freq == half, 0.0, 1.0)
            weight = jnp.where(freq == 0, 1.0, 2.0) * (scale / (2.0 * members * rows))
            work[freq, :, :rows] = weight * (lr + ones * ur)
            work[freq, :, rows:] = weight * (li - ones * ui)

            @pl.when(freq < half)
            def _():
                work[members - freq, :, :rows] = weight * (lr - ur)
                work[members - freq, :, rows:] = weight * (li + ui)

            return carry

        scale = norm if which == 2 else 1.0
        lax.fori_loop(0, half + 1, untwist, 0)

        def total_of(block, odd):
            total = jnp.zeros((chans, rows), f32)
            for freq in range(half + 1):
                place = members - freq if odd else freq
                total = total + cos_ref[freq, block] * work[place, :, :rows]
                total = total - sin_ref[freq, block] * work[place, :, rows:]
            return total

        def finish(step, carry):
            blocks = [step * 4 + place for place in range(4)]
            totals = [total_of(block, place % 2 == 1) for place, block in enumerate(blocks)]
            for block, total in zip(blocks, totals):
                top = row_top(total)
                back[which, block] = encode(total, top)
                back_tops[which, block] = to_lanes(top)
            for block in blocks:

                @pl.when(block != me)
                def _():
                    homeward(which, block, me).start()
                    homeward_top(which, block, me).start()

            return carry

        lax.fori_loop(0, members // 4, finish, 0)
        home[which, me] = back[which, me]
        home_tops[which, me] = back_tops[which, me]

    fwd_copy.wait()
    forward(0)
    forward(2)
    inv_copy.wait()
    inverse(1, 0, 2, -1.0)
    forward(1)
    inverse(0, 0, 1, 1.0)
    inverse(2, 1, 2, -1.0)

    def settle(which):
        homeward_top_all(which).wait_recv()
        homeward_all(which).wait_recv()
        for source in range(members):
            turned[which, source * chans : source * chans + chans, :] = decode(
                home[which, source], to_column(home_tops[which, source], chans)
            )

    before = lax.rem(me + members - 1, members)
    query_edge = remote(
        edge_out.at[0], edge_in.at[0], edge_sem.at[0], edge_sem.at[1], before
    )
    other_edges = remote(
        edge_out.at[pl.ds(1, 2)], edge_in.at[pl.ds(1, 2)], edge_sem.at[2], edge_sem.at[3], before
    )

    def gate_query(step, carry):
        here = pl.ds(pl.multiple_of(step * step_rows, step_rows), step_rows)
        mixed = grads[0, here, :]
        hyena_ref[here, :] = (features[0, here, :] * mixed).astype(jnp.bfloat16)
        grads[0, here, :] = cot_ref[here, :].astype(f32) * mixed
        return carry

    def gate_others(step, carry):
        here = pl.ds(pl.multiple_of(step * step_rows, step_rows), step_rows)
        grad_product = grads[1, here, :]
        grads[1, here, :] = grad_product * features[2, here, :]
        grads[2, here, :] = grad_product * features[1, here, :]
        return carry

    def all_taps(which):
        def tap_sums(step, carry):
            start = pl.multiple_of(step * step_rows, step_rows)
            window = extended[which, pl.ds(start, step_rows + edge), :]
            grad = grads[which, pl.ds(start, step_rows), :]
            return tuple(
                total
                + jnp.sum(
                    (grad * window[edge - tap : edge - tap + step_rows]).reshape(
                        step_rows // 8, 8, width
                    ),
                    axis=0,
                )
                for tap, total in enumerate(carry)
            )

        totals = lax.fori_loop(
            0, chunks, tap_sums, tuple(jnp.zeros((8, width), f32) for _ in range(taps))
        )
        lines = [jnp.sum(total, axis=0, keepdims=True) for total in totals]
        lines.append(jnp.zeros((8 - taps, width), f32))
        block = jnp.concatenate(lines, axis=0)
        for tile in range(lane_tiles):
            parts[which * lane_tiles + tile] = block[:, tile * 128 : tile * 128 + 128]

    def each_piece(body):
        def one(piece, carry):
            @pl.when(piece != me)
            def _():
                body(piece)

            return carry

        lax.fori_loop(0, pieces, one, 0)

    def back_taps(which):
        def one(step, carry):
            start = pl.multiple_of(step * step_rows, step_rows)
            window = grads[which, pl.ds(start, step_rows + edge), :]
            total = weight_ref[which, 0:1, :] * window[:step_rows]
            for tap in range(1, taps):
                total = total + weight_ref[which, tap : tap + 1, :] * window[tap : tap + step_rows]
            stream_grad_ref[which, pl.ds(start, step_rows), :] = total.astype(jnp.bfloat16)
            return carry

        lax.fori_loop(0, chunks, one, 0)

    @pl.when(me == members - 1)
    def _():
        grads[:, rows:, :] = jnp.zeros((3, edge, width), f32)

    settle(1)
    grads[1, :rows, :] = turned[1].T
    lax.fori_loop(0, chunks, gate_others, 0)
    edge_out[1:] = grads[1:, :edge, :]

    @pl.when(me > 0)
    def _():
        other_edges.start()

    all_taps(1)
    all_taps(2)

    @pl.when(me < members - 1)
    def _():
        other_edges.wait_recv()
        grads[1:, rows:, :] = edge_in[1:]

    back_taps(1)
    back_taps(2)
    settle(0)
    grads[0, :rows, :] = turned[0].T
    lax.fori_loop(0, chunks, gate_query, 0)
    edge_out[0] = grads[0, :edge, :]

    @pl.when(me > 0)
    def _():
        query_edge.start()

    all_taps(0)
    each_piece(lambda piece: part_out(piece, me).start())

    @pl.when(me < members - 1)
    def _():
        query_edge.wait_recv()
        grads[0, rows:, :] = edge_in[0]

    back_taps(0)

    @pl.when(me < pieces)
    def _():
        gathered[me] = parts[me]
        part_all.wait_recv()
        total = gathered[0]
        for source in range(1, members):
            total = total + gathered[source]
        sums[me] = total
        others(lambda other: sum_out(other, me).start())

    settle(2)
    filter_grad_ref[...] = turned[2].T

    each_piece(lambda piece: sum_out(piece, piece).wait_recv())
    for which in range(3):
        for tile in range(lane_tiles):
            short_ref[which, :, tile * 128 : tile * 128 + 128] = sums[which * lane_tiles + tile][
                :taps
            ]

    for which in range(3):
        outward_all(which).wait_send()
        homeward_all(which).wait_send()
        homeward_top_all(which).wait_send()
    outward_top_all.wait_send()
    each_piece(lambda piece: part_out(piece, me).wait_send())

    @pl.when(me < pieces)
    def _():
        sum_all.wait_send()

    @pl.when(me < members - 1)
    def _():
        halo_out.wait_send()

    @pl.when(me > 0)
    def _():
        query_edge.wait_send()
        other_edges.wait_send()


def tables(members, rows):
    period = 2 * members * rows
    coarse = np.outer(np.arange(members // 2 + 1), np.arange(members)) % (2 * members)
    coarse = coarse * (math.pi / members)
    twist = np.outer(np.arange(members + 1), np.arange(rows)) % period * (2.0 * math.pi / period)
    fine = np.outer(np.arange(rows), np.arange(rows)) % rows * (2.0 * math.pi / rows)
    c, s = np.cos(fine), np.sin(fine)
    forward = np.block([[c, -s], [s, c]])

    def split(matrix):
        high = matrix.astype(jnp.bfloat16)
        low = (matrix - high.astype(np.float64)).astype(jnp.bfloat16)
        return np.concatenate([high, high, low])

    return (
        np.cos(coarse).astype(np.float32),
        np.sin(coarse).astype(np.float32),
        np.stack([np.cos(twist), np.sin(twist)]).astype(np.float32),
        split(forward),
        split(forward.T),
    )


def hand_over(*refs):
    sem = refs[12]
    arrivals = [
        pltpu.make_async_copy(refs[place], refs[8 + place], sem.at[0, place]) for place in range(4)
    ]
    leaving = [
        pltpu.make_async_copy(refs[8 + place], refs[4 + place], sem.at[1, place])
        for place in range(4)
    ]
    for copy in arrivals:
        copy.start()
    for arrival, copy in zip(arrivals, leaving):
        arrival.wait()
        copy.start()
    for copy in leaving:
        copy.wait()


def on_device(streams, short_weight, long_filter, cotangent):
    members = lax.axis_size("ctx")
    rows, width = long_filter.shape
    chans = width // members
    pieces = 3 * (width // 128)
    norm = 1.0 / math.sqrt(rows * members)
    vmem = pl.BlockSpec(memory_space=pltpu.VMEM)
    smem = pl.BlockSpec(memory_space=pltpu.SMEM)
    wire = pltpu.VMEM((3, members, chans, rows), jnp.bfloat16)
    dma = pltpu.SemaphoreType.DMA
    results = tuple(
        pl.pallas_call(
            functools.partial(hyena_kernel, members, norm),
            out_shape=(
                jax.ShapeDtypeStruct((rows, width), jnp.bfloat16),
                jax.ShapeDtypeStruct(streams.shape, jnp.bfloat16),
                jax.ShapeDtypeStruct(short_weight.shape, f32),
                jax.ShapeDtypeStruct((rows, width), f32),
            ),
            in_specs=[vmem] * 4 + [smem] * 2 + [vmem] + [pl.BlockSpec(memory_space=pl.ANY)] * 2,
            out_specs=(vmem,) * 4,
            scratch_shapes=[
                pltpu.VMEM((3, width, rows), f32),
                wire,
                pltpu.VMEM((members, 1, 384), f32),
                wire,
                pltpu.VMEM((members, 1, 384), f32),
                wire,
                pltpu.VMEM((3, members, 1, 128), f32),
                wire,
                pltpu.VMEM((3, members, 1, 128), f32),
                pltpu.VMEM((members, chans, rows), f32),
                pltpu.VMEM((3, members + 1, chans, 2 * rows), f32),
                pltpu.VMEM((members + 1, chans, 2 * rows), f32),
                pltpu.VMEM((3, rows, width), f32),
                pltpu.VMEM((3, rows + edge, width), f32),
                pltpu.VMEM((3, rows + edge, width), f32),
                pltpu.VMEM((3, 16, width), jnp.bfloat16),
                pltpu.VMEM((3, edge, width), f32),
                pltpu.VMEM((3, edge, width), f32),
                pltpu.VMEM((pieces, 8, 128), f32),
                pltpu.VMEM((members, 8, 128), f32),
                pltpu.VMEM((pieces, 8, 128), f32),
                dma((3,)),
                dma((3,)),
                dma((1,)),
                dma((1,)),
                dma((3,)),
                dma((3,)),
                dma((3,)),
                dma((3,)),
                dma((2,)),
                dma((4,)),
                dma((pieces,)),
                dma((1,)),
                dma((1,)),
                dma((pieces,)),
                pltpu.VMEM((6 * rows, 2 * rows), jnp.bfloat16),
                pltpu.VMEM((6 * rows, 2 * rows), jnp.bfloat16),
                dma((2,)),
            ],
            compiler_params=pltpu.CompilerParams(
                collective_id=0, has_side_effects=True, vmem_limit_bytes=56 * 1024 * 1024
            ),
        )(
            streams, short_weight, long_filter, cotangent,
            *[jnp.asarray(t) for t in tables(members, rows)],
        )
    )
    anywhere = pl.BlockSpec(memory_space=pl.ANY)
    return tuple(
        pl.pallas_call(
            hand_over,
            out_shape=tuple(jax.ShapeDtypeStruct(r.shape, r.dtype) for r in results),
            in_specs=[anywhere] * 4,
            out_specs=(anywhere,) * 4,
            scratch_shapes=[pltpu.VMEM(r.shape, r.dtype) for r in results] + [dma((2, 4))],
            compiler_params=pltpu.CompilerParams(vmem_limit_bytes=60 * 1024 * 1024),
        )(*results)
    )


def solution(mesh):
    placed = (P(None, "ctx", "ch"), P(None, None, "ch"), P("ctx", "ch"), P("ctx", "ch"))
    return jax.shard_map(
        on_device,
        mesh=mesh,
        in_specs=placed,
        out_specs=(P("ctx", "ch"), P(None, "ctx", "ch"), P(None, None, "ch"), P("ctx", "ch")),
        check_vma=False,
    )
```

```python
import functools
import math

import jax
import jax.numpy as jnp
import numpy as np
from jax import lax
from jax.experimental import pallas as pl
from jax.experimental.pallas import tpu as pltpu
from jax.sharding import PartitionSpec as P

span = 250.0
half_span = 125.0
tiny = 1e-30
edge = 8
step_rows = 32
f32 = jnp.float32


def encode(values, top):
    power = jnp.abs(values) * (span / top) - half_span
    code = jnp.exp2(power)
    return jnp.where(values < 0.0, -code, code).astype(jnp.bfloat16)


def decode(code, top):
    code = code.astype(f32)
    size = (jnp.log2(jnp.abs(code)) + half_span) * (top * (1.0 / span))
    return jnp.where(code < 0.0, -size, size)


def row_top(values):
    return jnp.maximum(jnp.max(jnp.abs(values), axis=1, keepdims=True), tiny)


def to_lanes(column):
    rows = column.shape[0]
    lane = lax.broadcasted_iota(jnp.int32, (rows, 128), 1)
    row = lax.broadcasted_iota(jnp.int32, (rows, 128), 0)
    return jnp.sum(jnp.where(lane == row, column, 0.0), axis=0, keepdims=True)


def to_column(line, rows):
    lane = lax.broadcasted_iota(jnp.int32, (rows, 128), 1)
    row = lax.broadcasted_iota(jnp.int32, (rows, 128), 0)
    return jnp.sum(jnp.where(lane == row, line, 0.0), axis=1, keepdims=True)


def three_products(values, table_ref):
    high = values.astype(jnp.bfloat16)
    low = (values - high.astype(f32)).astype(jnp.bfloat16)
    return jnp.dot(
        jnp.concatenate([high, low, high], axis=1), table_ref[...], preferred_element_type=f32
    )


def feature_rows(extended_ref, weight_ref, which, start):
    taps = weight_ref.shape[1]
    window = extended_ref[which, pl.ds(start, step_rows + edge), :]
    total = weight_ref[which, 0:1, :] * window[edge : edge + step_rows]
    for tap in range(1, taps):
        total = total + weight_ref[which, tap : tap + 1, :] * window[edge - tap : edge - tap + step_rows]
    return total


def hyena_kernel(
    members, norm, streams_ref, weight_ref, filt_ref, cot_ref, cos_ref, sin_ref, twist_ref,
    fwd_any, inv_any,
    hyena_ref, stream_grad_ref, short_ref, filter_grad_ref,
    turned, packed, tops, got, got_tops, back, back_tops, home, home_tops,
    waves, spectra, work, folded, features, extended, grads, halo, edge_out, edge_in, parts, gathered, sums,
    send_sem, recv_sem, top_send, top_recv, back_send, back_recv, back_top_send, back_top_recv,
    halo_sem, edge_sem, part_send, part_recv, sum_send, sum_recv,
    fwd_ref, inv_ref, table_sem,
):
    me = lax.axis_index("ctx")
    mine = lax.axis_index("ch")
    rows, width = filt_ref.shape
    chans = width // members
    half = members // 2
    quarter = members // 4
    taps = weight_ref.shape[1]
    lane_tiles = width // 128
    pieces = 3 * lane_tiles
    chunks = rows // step_rows

    def remote(source, target, sent, received, other):
        return pltpu.make_async_remote_copy(
            src_ref=source, dst_ref=target, send_sem=sent, recv_sem=received,
            device_id=(other, mine), device_id_type=pl.DeviceIdType.MESH,
        )

    def others(body):
        if members <= 16:
            for step in range(1, members):
                body(lax.rem(me + step, members))
            return

        def one(step, carry):
            body(lax.rem(me + step, members))
            return carry

        lax.fori_loop(1, members, one, 0)

    def outward(which, other, source):
        return remote(
            packed.at[which, other], got.at[which, source],
            send_sem.at[which], recv_sem.at[which], other,
        )

    def outward_top(which, other, source):
        return remote(
            tops.at[which, other], got_tops.at[which, source],
            top_send.at[which], top_recv.at[which], other,
        )

    def homeward(which, other, source):
        return remote(
            back.at[which, other], home.at[which, source],
            back_send.at[which], back_recv.at[which], other,
        )

    def homeward_top(which, other, source):
        return remote(
            back_tops.at[which, other], home_tops.at[which, source],
            back_top_send.at[which], back_top_recv.at[which], other,
        )

    def part_out(piece, source):
        return remote(
            parts.at[piece], gathered.at[source], part_send.at[piece], part_recv.at[0], piece
        )

    def sum_out(other, piece):
        return remote(
            sums.at[piece], sums.at[piece], sum_send.at[0], sum_recv.at[piece], other
        )

    most = pl.ds(0, members - 1)
    near = lax.rem(me + 1, members)

    def outward_all(which):
        return remote(
            packed.at[which, most], got.at[which, most], send_sem.at[which], recv_sem.at[which], near
        )

    def homeward_all(which):
        return remote(
            back.at[which, most], home.at[which, most], back_send.at[which], back_recv.at[which], near
        )

    def outward_top_all(which):
        return remote(
            tops.at[which, most], got_tops.at[which, most],
            top_send.at[which], top_recv.at[which], near,
        )

    def homeward_top_all(which):
        return remote(
            back_tops.at[which, most], home_tops.at[which, most],
            back_top_send.at[which], back_top_recv.at[which], near,
        )

    part_all = remote(
        gathered.at[most], gathered.at[most], sum_send.at[0], part_recv.at[0], near
    )
    sum_all = remote(
        gathered.at[most], gathered.at[most], sum_send.at[0], part_recv.at[0], near
    )

    barrier = pltpu.get_barrier_semaphore()

    def greet(other):
        pl.semaphore_signal(
            barrier, inc=1, device_id=(other, mine), device_id_type=pl.DeviceIdType.MESH
        )

    others(greet)
    fwd_copy = pltpu.make_async_copy(fwd_any, fwd_ref, table_sem.at[0])
    inv_copy = pltpu.make_async_copy(inv_any, inv_ref, table_sem.at[1])
    fwd_copy.start()
    inv_copy.start()

    def pack(which, other):
        values = turned[which, other * chans : other * chans + chans, :]
        top = row_top(values)
        packed[which, other] = encode(values, top)
        tops[which, other] = to_lanes(top)

    def pack_all(which):
        for other in range(members):
            pack(which, other)

    halo_out = remote(
        streams_ref.at[:, pl.ds(rows - 16, 16), :], halo, halo_sem.at[0], halo_sem.at[1],
        lax.rem(me + 1, members),
    )
    turned[0] = filt_ref[...].T
    pack_all(0)
    pl.semaphore_wait(barrier, members - 1)

    @pl.when(me < members - 1)
    def _():
        halo_out.start()

    def send_out(which):
        others(lambda other: outward_top(which, other, me).start())
        others(lambda other: outward(which, other, me).start())
        got[which, me] = packed[which, me]
        got_tops[which, me] = tops[which, me]

    send_out(0)

    for which in range(3):
        extended[which, edge:, :] = streams_ref[which].astype(f32)

    @pl.when(me > 0)
    def _():
        halo_out.wait_recv()
        for which in range(3):
            extended[which, :edge, :] = halo[which].astype(f32)[16 - edge :]

    @pl.when(me == 0)
    def _():
        extended[:, :edge, :] = jnp.zeros((3, edge, width), f32)

    def featurize(step, carry):
        start = pl.multiple_of(step * step_rows, step_rows)
        query, key, value = [
            feature_rows(extended, weight_ref, which, start) for which in range(3)
        ]
        here = pl.ds(start, step_rows)
        features[0, here, :] = query
        features[1, here, :] = key
        features[2, here, :] = value
        grads[0, here, :] = key * value
        grads[1, here, :] = cot_ref[here, :].astype(f32) * query
        return carry

    lax.fori_loop(0, chunks, featurize, 0)
    turned[2] = grads[1, :rows, :].T
    pack_all(2)
    send_out(2)
    turned[1] = grads[0, :rows, :].T
    pack_all(1)
    send_out(1)

    height = (members + 1) * chans

    def forward(which):
        outward_top_all(which).wait_recv()
        outward_all(which).wait_recv()
        for source in range(members):
            top = to_column(got_tops[which, source], chans)
            if which == 0:
                top = top * norm
            waves[source] = decode(got[which, source], top)

        def coarse(freq, carry):
            sides = []
            for residue in range(4):
                real = jnp.zeros((chans, rows), f32)
                imag = jnp.zeros((chans, rows), f32)
                for block in range(residue, members, 4):
                    value = waves[block]
                    real = real + cos_ref[freq, block] * value
                    imag = imag - sin_ref[freq, block] * value
                sides.append((real, imag))
            (ar, ai), (br, bi), (cr, ci), (dr, di) = sides

            def put(place, real, imag):
                cosine = twist_ref[0, pl.ds(place, 1), :]
                sine = twist_ref[1, pl.ds(place, 1), :]
                spectra[which, place, :, :rows] = real * cosine + imag * sine
                spectra[which, place, :, rows:] = imag * cosine - real * sine

            put(freq, (ar + cr) + (br + dr), (ai + ci) + (bi + di))
            put(members - freq, (ar + cr) - (br + dr), (bi + di) - (ai + ci))
            put(half - freq, (ar - cr) - (bi - di), (ci - ai) - (br - dr))
            put(half + freq, (ar - cr) + (bi - di), (ai - ci) - (br - dr))
            return carry

        lax.fori_loop(0, quarter + 1, coarse, 0)
        flat = spectra[which].reshape(height, 2 * rows)
        spectra[which] = three_products(flat, fwd_ref).reshape(
            members + 1, chans, 2 * rows
        )

    def inverse(which, left, right, sign):
        def multiply(freq, carry):
            lr, li = spectra[left, freq, :, :rows], spectra[left, freq, :, rows:] * sign
            rr, ri = spectra[right, freq, :, :rows], spectra[right, freq, :, rows:]
            work[freq, :, :rows] = lr * rr - li * ri
            work[freq, :, rows:] = lr * ri + li * rr
            return carry

        lax.fori_loop(0, members + 1, multiply, 0)
        flat = work[...].reshape(height, 2 * rows)
        work[...] = three_products(flat, inv_ref).reshape(members + 1, chans, 2 * rows)

        def untwist(freq, carry):
            def turn(place):
                cosine = twist_ref[0, pl.ds(place, 1), :]
                sine = twist_ref[1, pl.ds(place, 1), :]
                real = work[place, :, :rows]
                imag = work[place, :, rows:]
                return real * cosine - imag * sine, imag * cosine + real * sine

            unit = scale / (2.0 * members * rows)
            first, last = freq == 0, freq == quarter
            outer = jnp.where(first, unit, 2.0 * unit)
            inner = jnp.where(last, 0.0, 2.0 * unit)
            upper = jnp.where(first, 0.0, inner)
            ar, ai = [outer * part for part in turn(freq)]
            br, bi = [outer * part for part in turn(members - freq)]
            cr, ci = [inner * part for part in turn(half - freq)]
            dr, di = [upper * part for part in turn(half + freq)]
            sums_r, diff_r = ar + br, ar - br
            sums_i, diff_i = ai + bi, ai - bi
            folded[0, freq, :, :rows] = sums_r + (cr + dr)
            folded[0, freq, :, rows:] = diff_i - (ci - di)
            folded[1, freq, :, :rows] = diff_r - (ci + di)
            folded[1, freq, :, rows:] = sums_i - (cr - dr)
            folded[2, freq, :, :rows] = sums_r - (cr + dr)
            folded[2, freq, :, rows:] = diff_i + (ci - di)
            folded[3, freq, :, :rows] = diff_r + (ci + di)
            folded[3, freq, :, rows:] = sums_i + (cr - dr)
            return carry

        scale = norm if which == 2 else 1.0
        lax.fori_loop(0, quarter + 1, untwist, 0)

        def total_of(block, residue):
            total = jnp.zeros((chans, rows), f32)
            for freq in range(quarter + 1):
                total = total + cos_ref[freq, block] * folded[residue, freq, :, :rows]
                total = total - sin_ref[freq, block] * folded[residue, freq, :, rows:]
            return total

        def finish(step, carry):
            blocks = [step * 4 + place for place in range(4)]
            totals = [total_of(block, place) for place, block in enumerate(blocks)]
            for block, total in zip(blocks, totals):
                top = row_top(total)
                back[which, block] = encode(total, top)
                back_tops[which, block] = to_lanes(top)
            for block in blocks:

                @pl.when(block != me)
                def _():
                    homeward(which, block, me).start()
                    homeward_top(which, block, me).start()

            return carry

        lax.fori_loop(0, members // 4, finish, 0)
        home[which, me] = back[which, me]
        home_tops[which, me] = back_tops[which, me]

    fwd_copy.wait()
    forward(0)
    forward(2)
    inv_copy.wait()
    inverse(1, 0, 2, -1.0)
    forward(1)
    inverse(0, 0, 1, 1.0)
    inverse(2, 1, 2, -1.0)

    def settle(which):
        homeward_top_all(which).wait_recv()
        homeward_all(which).wait_recv()
        for source in range(members):
            turned[which, source * chans : source * chans + chans, :] = decode(
                home[which, source], to_column(home_tops[which, source], chans)
            )

    before = lax.rem(me + members - 1, members)
    query_edge = remote(
        edge_out.at[0], edge_in.at[0], edge_sem.at[0], edge_sem.at[1], before
    )
    other_edges = remote(
        edge_out.at[pl.ds(1, 2)], edge_in.at[pl.ds(1, 2)], edge_sem.at[2], edge_sem.at[3], before
    )

    def gate_query(step, carry):
        here = pl.ds(pl.multiple_of(step * step_rows, step_rows), step_rows)
        mixed = grads[0, here, :]
        hyena_ref[here, :] = (features[0, here, :] * mixed).astype(jnp.bfloat16)
        grads[0, here, :] = cot_ref[here, :].astype(f32) * mixed
        return carry

    def gate_others(step, carry):
        here = pl.ds(pl.multiple_of(step * step_rows, step_rows), step_rows)
        grad_product = grads[1, here, :]
        grads[1, here, :] = grad_product * features[2, here, :]
        grads[2, here, :] = grad_product * features[1, here, :]
        return carry

    def all_taps(which):
        def tap_sums(step, carry):
            start = pl.multiple_of(step * step_rows, step_rows)
            window = extended[which, pl.ds(start, step_rows + edge), :]
            grad = grads[which, pl.ds(start, step_rows), :]
            return tuple(
                total
                + jnp.sum(
                    (grad * window[edge - tap : edge - tap + step_rows]).reshape(
                        step_rows // 8, 8, width
                    ),
                    axis=0,
                )
                for tap, total in enumerate(carry)
            )

        totals = lax.fori_loop(
            0, chunks, tap_sums, tuple(jnp.zeros((8, width), f32) for _ in range(taps))
        )
        lines = [jnp.sum(total, axis=0, keepdims=True) for total in totals]
        lines.append(jnp.zeros((8 - taps, width), f32))
        block = jnp.concatenate(lines, axis=0)
        for tile in range(lane_tiles):
            parts[which * lane_tiles + tile] = block[:, tile * 128 : tile * 128 + 128]

    def each_piece(body):
        def one(piece, carry):
            @pl.when(piece != me)
            def _():
                body(piece)

            return carry

        lax.fori_loop(0, pieces, one, 0)

    def back_taps(which):
        def one(step, carry):
            start = pl.multiple_of(step * step_rows, step_rows)
            window = grads[which, pl.ds(start, step_rows + edge), :]
            total = weight_ref[which, 0:1, :] * window[:step_rows]
            for tap in range(1, taps):
                total = total + weight_ref[which, tap : tap + 1, :] * window[tap : tap + step_rows]
            stream_grad_ref[which, pl.ds(start, step_rows), :] = total.astype(jnp.bfloat16)
            return carry

        lax.fori_loop(0, chunks, one, 0)

    @pl.when(me == members - 1)
    def _():
        grads[:, rows:, :] = jnp.zeros((3, edge, width), f32)

    settle(1)
    grads[1, :rows, :] = turned[1].T
    lax.fori_loop(0, chunks, gate_others, 0)
    edge_out[1:] = grads[1:, :edge, :]

    @pl.when(me > 0)
    def _():
        other_edges.start()

    all_taps(1)
    all_taps(2)

    @pl.when(me < members - 1)
    def _():
        other_edges.wait_recv()
        grads[1:, rows:, :] = edge_in[1:]

    back_taps(1)
    back_taps(2)
    settle(0)
    grads[0, :rows, :] = turned[0].T
    lax.fori_loop(0, chunks, gate_query, 0)
    edge_out[0] = grads[0, :edge, :]

    @pl.when(me > 0)
    def _():
        query_edge.start()

    all_taps(0)
    each_piece(lambda piece: part_out(piece, me).start())

    @pl.when(me < members - 1)
    def _():
        query_edge.wait_recv()
        grads[0, rows:, :] = edge_in[0]

    back_taps(0)

    @pl.when(me < pieces)
    def _():
        gathered[me] = parts[me]
        part_all.wait_recv()
        total = gathered[0]
        for source in range(1, members):
            total = total + gathered[source]
        sums[me] = total
        others(lambda other: sum_out(other, me).start())

    settle(2)
    filter_grad_ref[...] = turned[2].T

    each_piece(lambda piece: sum_out(piece, piece).wait_recv())
    for which in range(3):
        for tile in range(lane_tiles):
            short_ref[which, :, tile * 128 : tile * 128 + 128] = sums[which * lane_tiles + tile][
                :taps
            ]

    for which in range(3):
        outward_all(which).wait_send()
        homeward_all(which).wait_send()
        homeward_top_all(which).wait_send()
        outward_top_all(which).wait_send()
    each_piece(lambda piece: part_out(piece, me).wait_send())

    @pl.when(me < pieces)
    def _():
        sum_all.wait_send()

    @pl.when(me < members - 1)
    def _():
        halo_out.wait_send()

    @pl.when(me > 0)
    def _():
        query_edge.wait_send()
        other_edges.wait_send()


def tables(members, rows):
    period = 2 * members * rows
    coarse = np.outer(np.arange(members // 2 + 1), np.arange(members)) % (2 * members)
    coarse = coarse * (math.pi / members)
    twist = np.outer(np.arange(members + 1), np.arange(rows)) % period * (2.0 * math.pi / period)
    fine = np.outer(np.arange(rows), np.arange(rows)) % rows * (2.0 * math.pi / rows)
    c, s = np.cos(fine), np.sin(fine)
    forward = np.block([[c, -s], [s, c]])

    def split(matrix):
        high = matrix.astype(jnp.bfloat16)
        low = (matrix - high.astype(np.float64)).astype(jnp.bfloat16)
        return np.concatenate([high, high, low])

    return (
        np.cos(coarse).astype(np.float32),
        np.sin(coarse).astype(np.float32),
        np.stack([np.cos(twist), np.sin(twist)]).astype(np.float32),
        split(forward),
        split(forward.T),
    )


def hand_over(*refs):
    sem = refs[12]
    arrivals = [
        pltpu.make_async_copy(refs[place], refs[8 + place], sem.at[0, place]) for place in range(4)
    ]
    leaving = [
        pltpu.make_async_copy(refs[8 + place], refs[4 + place], sem.at[1, place])
        for place in range(4)
    ]
    for copy in arrivals:
        copy.start()
    for arrival, copy in zip(arrivals, leaving):
        arrival.wait()
        copy.start()
    for copy in leaving:
        copy.wait()


def on_device(streams, short_weight, long_filter, cotangent):
    members = lax.axis_size("ctx")
    rows, width = long_filter.shape
    chans = width // members
    pieces = 3 * (width // 128)
    norm = 1.0 / math.sqrt(rows * members)
    vmem = pl.BlockSpec(memory_space=pltpu.VMEM)
    smem = pl.BlockSpec(memory_space=pltpu.SMEM)
    wire = pltpu.VMEM((3, members, chans, rows), jnp.bfloat16)
    dma = pltpu.SemaphoreType.DMA
    results = tuple(
        pl.pallas_call(
            functools.partial(hyena_kernel, members, norm),
            out_shape=(
                jax.ShapeDtypeStruct((rows, width), jnp.bfloat16),
                jax.ShapeDtypeStruct(streams.shape, jnp.bfloat16),
                jax.ShapeDtypeStruct(short_weight.shape, f32),
                jax.ShapeDtypeStruct((rows, width), f32),
            ),
            in_specs=[vmem] * 4 + [smem] * 2 + [vmem] + [pl.BlockSpec(memory_space=pl.ANY)] * 2,
            out_specs=(vmem,) * 4,
            scratch_shapes=[
                pltpu.VMEM((3, width, rows), f32),
                wire,
                pltpu.VMEM((3, members, 1, 128), f32),
                wire,
                pltpu.VMEM((3, members, 1, 128), f32),
                wire,
                pltpu.VMEM((3, members, 1, 128), f32),
                wire,
                pltpu.VMEM((3, members, 1, 128), f32),
                pltpu.VMEM((members, chans, rows), f32),
                pltpu.VMEM((3, members + 1, chans, 2 * rows), f32),
                pltpu.VMEM((members + 1, chans, 2 * rows), f32),
                pltpu.VMEM((4, members // 4 + 1, chans, 2 * rows), f32),
                pltpu.VMEM((3, rows, width), f32),
                pltpu.VMEM((3, rows + edge, width), f32),
                pltpu.VMEM((3, rows + edge, width), f32),
                pltpu.VMEM((3, 16, width), jnp.bfloat16),
                pltpu.VMEM((3, edge, width), f32),
                pltpu.VMEM((3, edge, width), f32),
                pltpu.VMEM((pieces, 8, 128), f32),
                pltpu.VMEM((members, 8, 128), f32),
                pltpu.VMEM((pieces, 8, 128), f32),
                dma((3,)),
                dma((3,)),
                dma((3,)),
                dma((3,)),
                dma((3,)),
                dma((3,)),
                dma((3,)),
                dma((3,)),
                dma((2,)),
                dma((4,)),
                dma((pieces,)),
                dma((1,)),
                dma((1,)),
                dma((pieces,)),
                pltpu.VMEM((6 * rows, 2 * rows), jnp.bfloat16),
                pltpu.VMEM((6 * rows, 2 * rows), jnp.bfloat16),
                dma((2,)),
            ],
            compiler_params=pltpu.CompilerParams(
                collective_id=0, has_side_effects=True, vmem_limit_bytes=56 * 1024 * 1024
            ),
        )(
            streams, short_weight, long_filter, cotangent,
            *[jnp.asarray(t) for t in tables(members, rows)],
        )
    )
    anywhere = pl.BlockSpec(memory_space=pl.ANY)
    return tuple(
        pl.pallas_call(
            hand_over,
            out_shape=tuple(jax.ShapeDtypeStruct(r.shape, r.dtype) for r in results),
            in_specs=[anywhere] * 4,
            out_specs=(anywhere,) * 4,
            scratch_shapes=[pltpu.VMEM(r.shape, r.dtype) for r in results] + [dma((2, 4))],
            compiler_params=pltpu.CompilerParams(vmem_limit_bytes=60 * 1024 * 1024),
        )(*results)
    )


def solution(mesh):
    placed = (P(None, "ctx", "ch"), P(None, None, "ch"), P("ctx", "ch"), P("ctx", "ch"))
    return jax.shard_map(
        on_device,
        mesh=mesh,
        in_specs=placed,
        out_specs=(P("ctx", "ch"), P(None, "ctx", "ch"), P(None, None, "ch"), P("ctx", "ch")),
        check_vma=False,
    )
```

```python
import functools
import math

import jax
import jax.numpy as jnp
import numpy as np
from jax import lax
from jax.experimental import pallas as pl
from jax.experimental.pallas import tpu as pltpu
from jax.sharding import PartitionSpec as P

span = 250.0 * math.log(2.0)
half_span = 0.5 * span
tiny = 1e-30
edge = 8
step_rows = 32
f32 = jnp.float32


def encode(values, top):
    power = jnp.abs(values) * (span / top) - half_span
    code = jnp.exp(power)
    return jnp.where(values < 0.0, -code, code).astype(jnp.bfloat16)


def decode(code, top):
    code = code.astype(f32)
    size = (jnp.log(jnp.abs(code)) + half_span) * (top * (1.0 / span))
    return jnp.where(code < 0.0, -size, size)


def row_top(values):
    return jnp.maximum(jnp.max(jnp.abs(values), axis=1, keepdims=True), tiny)


def to_lanes(column):
    rows = column.shape[0]
    lane = lax.broadcasted_iota(jnp.int32, (rows, 128), 1)
    row = lax.broadcasted_iota(jnp.int32, (rows, 128), 0)
    return jnp.sum(jnp.where(lane == row, column, 0.0), axis=0, keepdims=True)


def to_column(line, rows):
    lane = lax.broadcasted_iota(jnp.int32, (rows, 128), 1)
    row = lax.broadcasted_iota(jnp.int32, (rows, 128), 0)
    return jnp.sum(jnp.where(lane == row, line, 0.0), axis=1, keepdims=True)


def three_products(values, table_ref):
    high = values.astype(jnp.bfloat16)
    low = (values - high.astype(f32)).astype(jnp.bfloat16)
    return jnp.dot(
        jnp.concatenate([high, low, high], axis=1), table_ref[...], preferred_element_type=f32
    )


def feature_rows(extended_ref, weight_ref, which, start):
    taps = weight_ref.shape[1]
    window = extended_ref[which, pl.ds(start, step_rows + edge), :]
    total = weight_ref[which, 0:1, :] * window[edge : edge + step_rows]
    for tap in range(1, taps):
        total = total + weight_ref[which, tap : tap + 1, :] * window[edge - tap : edge - tap + step_rows]
    return total


def hyena_kernel(
    members, norm, streams_ref, weight_ref, filt_ref, cot_ref, cos_ref, sin_ref, twist_ref,
    fwd_any, inv_any,
    hyena_ref, stream_grad_ref, short_ref, filter_grad_ref,
    turned, packed, tops, got, got_tops, back, back_tops, home, home_tops,
    waves, spectra, work, folded, features, extended, grads, halo, edge_out, edge_in, parts, gathered, sums,
    send_sem, recv_sem, top_send, top_recv, back_send, back_recv, back_top_send, back_top_recv,
    halo_sem, edge_sem, part_send, part_recv, sum_send, sum_recv,
    fwd_ref, inv_ref, table_sem,
):
    me = lax.axis_index("ctx")
    mine = lax.axis_index("ch")
    rows, width = filt_ref.shape
    chans = width // members
    half = members // 2
    quarter = members // 4
    taps = weight_ref.shape[1]
    lane_tiles = width // 128
    pieces = 3 * lane_tiles
    chunks = rows // step_rows

    def remote(source, target, sent, received, other):
        return pltpu.make_async_remote_copy(
            src_ref=source, dst_ref=target, send_sem=sent, recv_sem=received,
            device_id=(other, mine), device_id_type=pl.DeviceIdType.MESH,
        )

    def others(body):
        if members <= 16:
            for step in range(1, members):
                body(lax.rem(me + step, members))
            return

        def one(step, carry):
            body(lax.rem(me + step, members))
            return carry

        lax.fori_loop(1, members, one, 0)

    def outward(which, other, source):
        return remote(
            packed.at[which, other], got.at[which, source],
            send_sem.at[which], recv_sem.at[which], other,
        )

    def outward_top(which, other, source):
        return remote(
            tops.at[which, other], got_tops.at[which, source],
            top_send.at[which], top_recv.at[which], other,
        )

    def homeward(which, other, source):
        return remote(
            back.at[which, other], home.at[which, source],
            back_send.at[which], back_recv.at[which], other,
        )

    def homeward_top(which, other, source):
        return remote(
            back_tops.at[which, other], home_tops.at[which, source],
            back_top_send.at[which], back_top_recv.at[which], other,
        )

    def part_out(piece, source):
        return remote(
            parts.at[piece], gathered.at[source], part_send.at[piece], part_recv.at[0], piece
        )

    def sum_out(other, piece):
        return remote(
            sums.at[piece], sums.at[piece], sum_send.at[0], sum_recv.at[piece], other
        )

    most = pl.ds(0, members - 1)
    near = lax.rem(me + 1, members)

    def outward_all(which):
        return remote(
            packed.at[which, most], got.at[which, most], send_sem.at[which], recv_sem.at[which], near
        )

    def homeward_all(which):
        return remote(
            back.at[which, most], home.at[which, most], back_send.at[which], back_recv.at[which], near
        )

    def outward_top_all(which):
        return remote(
            tops.at[which, most], got_tops.at[which, most],
            top_send.at[which], top_recv.at[which], near,
        )

    def homeward_top_all(which):
        return remote(
            back_tops.at[which, most], home_tops.at[which, most],
            back_top_send.at[which], back_top_recv.at[which], near,
        )

    part_all = remote(
        gathered.at[most], gathered.at[most], sum_send.at[0], part_recv.at[0], near
    )
    sum_all = remote(
        gathered.at[most], gathered.at[most], sum_send.at[0], part_recv.at[0], near
    )

    barrier = pltpu.get_barrier_semaphore()

    def greet(other):
        pl.semaphore_signal(
            barrier, inc=1, device_id=(other, mine), device_id_type=pl.DeviceIdType.MESH
        )

    others(greet)
    fwd_copy = pltpu.make_async_copy(fwd_any, fwd_ref, table_sem.at[0])
    inv_copy = pltpu.make_async_copy(inv_any, inv_ref, table_sem.at[1])
    fwd_copy.start()
    inv_copy.start()

    def pack(which, other):
        values = turned[which, other * chans : other * chans + chans, :]
        top = row_top(values)
        packed[which, other] = encode(values, top)
        tops[which, other] = to_lanes(top)

    def pack_all(which):
        for other in range(members):
            pack(which, other)

    halo_out = remote(
        streams_ref.at[:, pl.ds(rows - 16, 16), :], halo, halo_sem.at[0], halo_sem.at[1],
        lax.rem(me + 1, members),
    )
    turned[0] = filt_ref[...].T
    pack_all(0)
    pl.semaphore_wait(barrier, members - 1)

    @pl.when(me < members - 1)
    def _():
        halo_out.start()

    def send_out(which):
        others(lambda other: outward_top(which, other, me).start())
        others(lambda other: outward(which, other, me).start())
        got[which, me] = packed[which, me]
        got_tops[which, me] = tops[which, me]

    send_out(0)

    for which in range(3):
        extended[which, edge:, :] = streams_ref[which].astype(f32)

    def featurize(step, carry):
        start = step * step_rows
        start = start if isinstance(step, int) else pl.multiple_of(start, step_rows)
        query, key, value = [
            feature_rows(extended, weight_ref, which, start) for which in range(3)
        ]
        here = pl.ds(start, step_rows)
        features[0, here, :] = query
        features[1, here, :] = key
        features[2, here, :] = value
        grads[0, here, :] = key * value
        grads[1, here, :] = cot_ref[here, :].astype(f32) * query
        return carry

    lax.fori_loop(1, chunks, featurize, 0)

    @pl.when(me > 0)
    def _():
        halo_out.wait_recv()
        for which in range(3):
            extended[which, :edge, :] = halo[which].astype(f32)[16 - edge :]

    @pl.when(me == 0)
    def _():
        extended[:, :edge, :] = jnp.zeros((3, edge, width), f32)

    featurize(0, 0)
    turned[2] = grads[1, :rows, :].T
    pack_all(2)
    send_out(2)
    turned[1] = grads[0, :rows, :].T
    pack_all(1)
    send_out(1)

    height = (members + 1) * chans

    def forward(which):
        outward_top_all(which).wait_recv()
        outward_all(which).wait_recv()
        for source in range(members):
            top = to_column(got_tops[which, source], chans)
            if which == 0:
                top = top * norm
            waves[source] = decode(got[which, source], top)

        def coarse(freq, carry):
            sides = []
            for residue in range(4):
                real = jnp.zeros((chans, rows), f32)
                imag = jnp.zeros((chans, rows), f32)
                for block in range(residue, members, 4):
                    value = waves[block]
                    real = real + cos_ref[freq, block] * value
                    imag = imag - sin_ref[freq, block] * value
                sides.append((real, imag))
            (ar, ai), (br, bi), (cr, ci), (dr, di) = sides

            def put(place, real, imag):
                cosine = twist_ref[0, pl.ds(place, 1), :]
                sine = twist_ref[1, pl.ds(place, 1), :]
                spectra[which, place, :, :rows] = real * cosine + imag * sine
                spectra[which, place, :, rows:] = imag * cosine - real * sine

            put(freq, (ar + cr) + (br + dr), (ai + ci) + (bi + di))
            put(members - freq, (ar + cr) - (br + dr), (bi + di) - (ai + ci))
            put(half - freq, (ar - cr) - (bi - di), (ci - ai) - (br - dr))
            put(half + freq, (ar - cr) + (bi - di), (ai - ci) - (br - dr))
            return carry

        lax.fori_loop(0, quarter + 1, coarse, 0)
        flat = spectra[which].reshape(height, 2 * rows)
        spectra[which] = three_products(flat, fwd_ref).reshape(
            members + 1, chans, 2 * rows
        )

    def inverse(which, left, right, sign):
        def multiply(freq, carry):
            lr, li = spectra[left, freq, :, :rows], spectra[left, freq, :, rows:] * sign
            rr, ri = spectra[right, freq, :, :rows], spectra[right, freq, :, rows:]
            work[freq, :, :rows] = lr * rr - li * ri
            work[freq, :, rows:] = lr * ri + li * rr
            return carry

        lax.fori_loop(0, members + 1, multiply, 0)
        flat = work[...].reshape(height, 2 * rows)
        work[...] = three_products(flat, inv_ref).reshape(members + 1, chans, 2 * rows)

        def untwist(freq, carry):
            def turn(place):
                cosine = twist_ref[0, pl.ds(place, 1), :]
                sine = twist_ref[1, pl.ds(place, 1), :]
                real = work[place, :, :rows]
                imag = work[place, :, rows:]
                return real * cosine - imag * sine, imag * cosine + real * sine

            unit = scale / (2.0 * members * rows)
            first, last = freq == 0, freq == quarter
            outer = jnp.where(first, unit, 2.0 * unit)
            inner = jnp.where(last, 0.0, 2.0 * unit)
            upper = jnp.where(first, 0.0, inner)
            ar, ai = [outer * part for part in turn(freq)]
            br, bi = [outer * part for part in turn(members - freq)]
            cr, ci = [inner * part for part in turn(half - freq)]
            dr, di = [upper * part for part in turn(half + freq)]
            sums_r, diff_r = ar + br, ar - br
            sums_i, diff_i = ai + bi, ai - bi
            folded[0, freq, :, :rows] = sums_r + (cr + dr)
            folded[0, freq, :, rows:] = diff_i - (ci - di)
            folded[1, freq, :, :rows] = diff_r - (ci + di)
            folded[1, freq, :, rows:] = sums_i - (cr - dr)
            folded[2, freq, :, :rows] = sums_r - (cr + dr)
            folded[2, freq, :, rows:] = diff_i + (ci - di)
            folded[3, freq, :, :rows] = diff_r + (ci + di)
            folded[3, freq, :, rows:] = sums_i + (cr - dr)
            return carry

        scale = norm if which == 2 else 1.0
        lax.fori_loop(0, quarter + 1, untwist, 0)

        def total_of(block, residue):
            total = jnp.zeros((chans, rows), f32)
            for freq in range(quarter + 1):
                total = total + cos_ref[freq, block] * folded[residue, freq, :, :rows]
                total = total - sin_ref[freq, block] * folded[residue, freq, :, rows:]
            return total

        def finish(step, carry):
            blocks = [step * 4 + place for place in range(4)]
            totals = [total_of(block, place) for place, block in enumerate(blocks)]
            for block, total in zip(blocks, totals):
                top = row_top(total)
                back[which, block] = encode(total, top)
                back_tops[which, block] = to_lanes(top)
            for block in blocks:

                @pl.when(block != me)
                def _():
                    homeward(which, block, me).start()
                    homeward_top(which, block, me).start()

            return carry

        lax.fori_loop(0, members // 4, finish, 0)
        home[which, me] = back[which, me]
        home_tops[which, me] = back_tops[which, me]

    fwd_copy.wait()
    forward(0)
    forward(2)
    inv_copy.wait()
    inverse(1, 0, 2, -1.0)
    forward(1)
    inverse(0, 0, 1, 1.0)
    inverse(2, 1, 2, -1.0)

    def settle(which):
        homeward_top_all(which).wait_recv()
        homeward_all(which).wait_recv()
        for source in range(members):
            turned[which, source * chans : source * chans + chans, :] = decode(
                home[which, source], to_column(home_tops[which, source], chans)
            )

    before = lax.rem(me + members - 1, members)
    query_edge = remote(
        edge_out.at[0], edge_in.at[0], edge_sem.at[0], edge_sem.at[1], before
    )
    other_edges = remote(
        edge_out.at[pl.ds(1, 2)], edge_in.at[pl.ds(1, 2)], edge_sem.at[2], edge_sem.at[3], before
    )

    def gate_query(step, carry):
        here = pl.ds(pl.multiple_of(step * step_rows, step_rows), step_rows)
        mixed = grads[0, here, :]
        hyena_ref[here, :] = (features[0, here, :] * mixed).astype(jnp.bfloat16)
        grads[0, here, :] = cot_ref[here, :].astype(f32) * mixed
        return carry

    def gate_others(step, carry):
        here = pl.ds(pl.multiple_of(step * step_rows, step_rows), step_rows)
        grad_product = grads[1, here, :]
        grads[1, here, :] = grad_product * features[2, here, :]
        grads[2, here, :] = grad_product * features[1, here, :]
        return carry

    def all_taps(which):
        def tap_sums(step, carry):
            start = pl.multiple_of(step * step_rows, step_rows)
            window = extended[which, pl.ds(start, step_rows + edge), :]
            grad = grads[which, pl.ds(start, step_rows), :]
            return tuple(
                total
                + jnp.sum(
                    (grad * window[edge - tap : edge - tap + step_rows]).reshape(
                        step_rows // 8, 8, width
                    ),
                    axis=0,
                )
                for tap, total in enumerate(carry)
            )

        totals = lax.fori_loop(
            0, chunks, tap_sums, tuple(jnp.zeros((8, width), f32) for _ in range(taps))
        )
        lines = [jnp.sum(total, axis=0, keepdims=True) for total in totals]
        lines.append(jnp.zeros((8 - taps, width), f32))
        block = jnp.concatenate(lines, axis=0)
        for tile in range(lane_tiles):
            parts[which * lane_tiles + tile] = block[:, tile * 128 : tile * 128 + 128]

    def each_piece(body):
        def one(piece, carry):
            @pl.when(piece != me)
            def _():
                body(piece)

            return carry

        lax.fori_loop(0, pieces, one, 0)

    def back_taps(which, begin, end):
        def one(step, carry):
            start = pl.multiple_of(step * step_rows, step_rows)
            window = grads[which, pl.ds(start, step_rows + edge), :]
            total = weight_ref[which, 0:1, :] * window[:step_rows]
            for tap in range(1, taps):
                total = total + weight_ref[which, tap : tap + 1, :] * window[tap : tap + step_rows]
            stream_grad_ref[which, pl.ds(start, step_rows), :] = total.astype(jnp.bfloat16)
            return carry

        lax.fori_loop(begin, end, one, 0)

    @pl.when(me == members - 1)
    def _():
        grads[:, rows:, :] = jnp.zeros((3, edge, width), f32)

    settle(1)
    grads[1, :rows, :] = turned[1].T
    lax.fori_loop(0, chunks, gate_others, 0)
    edge_out[1:] = grads[1:, :edge, :]

    @pl.when(me > 0)
    def _():
        other_edges.start()

    all_taps(1)
    all_taps(2)
    back_taps(1, 0, chunks - 1)
    back_taps(2, 0, chunks - 1)

    @pl.when(me < members - 1)
    def _():
        other_edges.wait_recv()
        grads[1:, rows:, :] = edge_in[1:]

    back_taps(1, chunks - 1, chunks)
    back_taps(2, chunks - 1, chunks)
    settle(0)
    grads[0, :rows, :] = turned[0].T
    lax.fori_loop(0, chunks, gate_query, 0)
    edge_out[0] = grads[0, :edge, :]

    @pl.when(me > 0)
    def _():
        query_edge.start()

    all_taps(0)
    each_piece(lambda piece: part_out(piece, me).start())
    back_taps(0, 0, chunks - 1)

    @pl.when(me < members - 1)
    def _():
        query_edge.wait_recv()
        grads[0, rows:, :] = edge_in[0]

    back_taps(0, chunks - 1, chunks)

    @pl.when(me < pieces)
    def _():
        gathered[me] = parts[me]
        part_all.wait_recv()
        total = gathered[0]
        for source in range(1, members):
            total = total + gathered[source]
        sums[me] = total
        others(lambda other: sum_out(other, me).start())

    settle(2)
    filter_grad_ref[...] = turned[2].T

    each_piece(lambda piece: sum_out(piece, piece).wait_recv())
    for which in range(3):
        for tile in range(lane_tiles):
            short_ref[which, :, tile * 128 : tile * 128 + 128] = sums[which * lane_tiles + tile][
                :taps
            ]

    for which in range(3):
        outward_all(which).wait_send()
        homeward_all(which).wait_send()
        homeward_top_all(which).wait_send()
        outward_top_all(which).wait_send()
    each_piece(lambda piece: part_out(piece, me).wait_send())

    @pl.when(me < pieces)
    def _():
        sum_all.wait_send()

    @pl.when(me < members - 1)
    def _():
        halo_out.wait_send()

    @pl.when(me > 0)
    def _():
        query_edge.wait_send()
        other_edges.wait_send()


def tables(members, rows):
    period = 2 * members * rows
    coarse = np.outer(np.arange(members // 2 + 1), np.arange(members)) % (2 * members)
    coarse = coarse * (math.pi / members)
    twist = np.outer(np.arange(members + 1), np.arange(rows)) % period * (2.0 * math.pi / period)
    fine = np.outer(np.arange(rows), np.arange(rows)) % rows * (2.0 * math.pi / rows)
    c, s = np.cos(fine), np.sin(fine)
    forward = np.block([[c, -s], [s, c]])

    def split(matrix):
        high = matrix.astype(jnp.bfloat16)
        low = (matrix - high.astype(np.float64)).astype(jnp.bfloat16)
        return np.concatenate([high, high, low])

    return (
        np.cos(coarse).astype(np.float32),
        np.sin(coarse).astype(np.float32),
        np.stack([np.cos(twist), np.sin(twist)]).astype(np.float32),
        split(forward),
        split(forward.T),
    )


def hand_over(*refs):
    sem = refs[12]
    arrivals = [
        pltpu.make_async_copy(refs[place], refs[8 + place], sem.at[0, place]) for place in range(4)
    ]
    leaving = [
        pltpu.make_async_copy(refs[8 + place], refs[4 + place], sem.at[1, place])
        for place in range(4)
    ]
    for copy in arrivals:
        copy.start()
    for arrival, copy in zip(arrivals, leaving):
        arrival.wait()
        copy.start()
    for copy in leaving:
        copy.wait()


def on_device(streams, short_weight, long_filter, cotangent):
    members = lax.axis_size("ctx")
    rows, width = long_filter.shape
    chans = width // members
    pieces = 3 * (width // 128)
    norm = 1.0 / math.sqrt(rows * members)
    vmem = pl.BlockSpec(memory_space=pltpu.VMEM)
    smem = pl.BlockSpec(memory_space=pltpu.SMEM)
    wire = pltpu.VMEM((3, members, chans, rows), jnp.bfloat16)
    dma = pltpu.SemaphoreType.DMA
    results = tuple(
        pl.pallas_call(
            functools.partial(hyena_kernel, members, norm),
            out_shape=(
                jax.ShapeDtypeStruct((rows, width), jnp.bfloat16),
                jax.ShapeDtypeStruct(streams.shape, jnp.bfloat16),
                jax.ShapeDtypeStruct(short_weight.shape, f32),
                jax.ShapeDtypeStruct((rows, width), f32),
            ),
            in_specs=[vmem] * 4 + [smem] * 2 + [vmem] + [pl.BlockSpec(memory_space=pl.ANY)] * 2,
            out_specs=(vmem,) * 4,
            scratch_shapes=[
                pltpu.VMEM((3, width, rows), f32),
                wire,
                pltpu.VMEM((3, members, 1, 128), f32),
                wire,
                pltpu.VMEM((3, members, 1, 128), f32),
                wire,
                pltpu.VMEM((3, members, 1, 128), f32),
                wire,
                pltpu.VMEM((3, members, 1, 128), f32),
                pltpu.VMEM((members, chans, rows), f32),
                pltpu.VMEM((3, members + 1, chans, 2 * rows), f32),
                pltpu.VMEM((members + 1, chans, 2 * rows), f32),
                pltpu.VMEM((4, members // 4 + 1, chans, 2 * rows), f32),
                pltpu.VMEM((3, rows, width), f32),
                pltpu.VMEM((3, rows + edge, width), f32),
                pltpu.VMEM((3, rows + edge, width), f32),
                pltpu.VMEM((3, 16, width), jnp.bfloat16),
                pltpu.VMEM((3, edge, width), f32),
                pltpu.VMEM((3, edge, width), f32),
                pltpu.VMEM((pieces, 8, 128), f32),
                pltpu.VMEM((members, 8, 128), f32),
                pltpu.VMEM((pieces, 8, 128), f32),
                dma((3,)),
                dma((3,)),
                dma((3,)),
                dma((3,)),
                dma((3,)),
                dma((3,)),
                dma((3,)),
                dma((3,)),
                dma((2,)),
                dma((4,)),
                dma((pieces,)),
                dma((1,)),
                dma((1,)),
                dma((pieces,)),
                pltpu.VMEM((6 * rows, 2 * rows), jnp.bfloat16),
                pltpu.VMEM((6 * rows, 2 * rows), jnp.bfloat16),
                dma((2,)),
            ],
            compiler_params=pltpu.CompilerParams(
                collective_id=0, has_side_effects=True, vmem_limit_bytes=56 * 1024 * 1024
            ),
        )(
            streams, short_weight, long_filter, cotangent,
            *[jnp.asarray(t) for t in tables(members, rows)],
        )
    )
    anywhere = pl.BlockSpec(memory_space=pl.ANY)
    return tuple(
        pl.pallas_call(
            hand_over,
            out_shape=tuple(jax.ShapeDtypeStruct(r.shape, r.dtype) for r in results),
            in_specs=[anywhere] * 4,
            out_specs=(anywhere,) * 4,
            scratch_shapes=[pltpu.VMEM(r.shape, r.dtype) for r in results] + [dma((2, 4))],
            compiler_params=pltpu.CompilerParams(vmem_limit_bytes=60 * 1024 * 1024),
        )(*results)
    )


def solution(mesh):
    placed = (P(None, "ctx", "ch"), P(None, None, "ch"), P("ctx", "ch"), P("ctx", "ch"))
    return jax.shard_map(
        on_device,
        mesh=mesh,
        in_specs=placed,
        out_specs=(P("ctx", "ch"), P(None, "ctx", "ch"), P(None, None, "ch"), P("ctx", "ch")),
        check_vma=False,
    )
```
